256 devices in a mesh: blk: 64 (over z, y_lo, x), rep: 4 (over y_hi, core).
Axes of the slice: x: 4, y: 4 (y_hi: 2, y_lo: 2; y = y_hi * 2 + y_lo), z: 8, core: 2. Of those that a mesh axis runs over, the one named last changes fastest.
Arguments:
- picture_vectors: bfloat16 [49152, 1152], P('blk'), may hold values from -0.1796875 to 0.1796875
- caption_vectors: bfloat16 [49152, 1152], P(('blk', 'rep')), may hold values from -0.1796875 to 0.1796875
- scale_exponent: float32 [1], replicated, may hold values from 1.5 to 2.5
- offset_addend: float32 [1], replicated, may hold values from -3 to -1
Outputs:
- grad_images: float32 [49152, 1152], P(('blk', 'rep'))
- grad_texts: float32 [49152, 1152], P(('blk', 'rep'))
- loss_rows: float32 [49152], P(('blk', 'rep'))
The draws below stay inside these ranges and needn't reach their ends.
All inputs are finite; a program needn't handle non-finite values.
Results may differ from the reference program's by a relative error of at most 0.015.
Values may be sent and summed in bfloat16 or wider, within the bound.
No kernel may reach another device: no remote copies, remote signals or barrier semaphores. Data moves between devices by JAX's collectives and lax.ppermute only.
A program may use at most 64 MiB of HBM per device.

```python
import jax
import jax.numpy as jnp
from jax import lax

D = 1152
BLOCK_ROWS = 768
BATCH = 49152
REACH_UP = 6
REACH_DOWN = 5
WINDOW = 12
N_BLK = 64


def levels(stream_key, shape, cuts, smallest, largest):
    loudness = 1.0
    for position, shards_of in cuts:
        heights = jax.random.uniform(jax.random.fold_in(jax.random.fold_in(stream_key, 6), position), (shards_of,), jnp.float32, smallest / len(cuts), largest / len(cuts))
        loudness = loudness * jnp.repeat(jnp.exp(heights), shape[position] // shards_of).reshape((-1,) + (1,) * (len(shape) - 1 - position))
    return loudness


def centred(stream_key, dims, spread, most, cuts=(), dtype=jnp.bfloat16):
    values = spread * jax.random.normal(stream_key, dims, jnp.float32)
    if cuts:
        values = values * levels(stream_key, dims, cuts, -0.22, 0.18)
    return jnp.clip(values, -most, most).astype(dtype)


def setup_inputs(seed: int = 0) -> dict:
    key_of = jax.random.split(jax.random.key(seed), 5)
    picture_vectors = centred(key_of[0], (BATCH, D), 0.03, 0.1796875, ((0, 64),))
    caption_vectors = centred(key_of[1], (BATCH, D), 0.03, 0.1796875, ((0, 256),))
    scale_exponent = jnp.clip(jax.random.uniform(key_of[2], (1,), jnp.float32, 1.5, 2.5), 1.5, 2.5)
    offset_addend = jnp.clip(jax.random.uniform(key_of[3], (1,), jnp.float32, -3.0, -1.0), -3.0, -1.0)
    return dict(picture_vectors=picture_vectors, caption_vectors=caption_vectors, scale_exponent=scale_exponent, offset_addend=offset_addend)


epsilon = 1e-06

def unit_rows(values):
    wide = values.astype(jnp.float32)
    norms = jnp.sqrt(lax.optimization_barrier(jnp.sum(wide * wide, axis=1, keepdims=True)) + epsilon)
    return (wide / norms, norms)

def reference(picture_vectors, caption_vectors, scale_exponent, offset_addend):
    affinity_multiplier = jnp.exp(scale_exponent[0])
    affinity_addend = offset_addend[0]
    image_unit, image_norm = unit_rows(picture_vectors)
    text_unit, text_norm = unit_rows(caption_vectors)
    picture_reduced_floats = lax.optimization_barrier(image_unit.astype(jnp.bfloat16)).astype(jnp.float32)
    caption_reduced_floats = lax.optimization_barrier(text_unit.astype(jnp.bfloat16)).astype(jnp.float32)
    picture_tile_sequence = picture_reduced_floats.reshape(N_BLK, BLOCK_ROWS, D)
    text_blocks = caption_reduced_floats.reshape(N_BLK, BLOCK_ROWS, D)
    diagonal = jnp.arange(BLOCK_ROWS)[:, None] == jnp.arange(BLOCK_ROWS)[None, :]
    losses = jnp.zeros((N_BLK, BLOCK_ROWS), jnp.float32)
    picture_direction_derivative = jnp.zeros((N_BLK, BLOCK_ROWS, D), jnp.float32)
    grad_text_unit = jnp.zeros((N_BLK, BLOCK_ROWS, D), jnp.float32)
    for offset in range(-REACH_DOWN, REACH_UP + 1):
        cycled_tiles = jnp.roll(text_blocks, offset, axis=0)
        cosine_affinities = jnp.einsum('vxr,vur->vxu', picture_tile_sequence, cycled_tiles)
        coupling_affinity_table = affinity_multiplier * cosine_affinities + affinity_addend
        if offset == 0:
            signs = jnp.where(diagonal, 1.0, -1.0).astype(jnp.float32)
        else:
            signs = -jnp.ones((BLOCK_ROWS, BLOCK_ROWS), jnp.float32)
        losses = losses - lax.optimization_barrier(jnp.sum(jax.nn.log_sigmoid(signs * coupling_affinity_table), axis=2))
        squashing_derivatives = (-signs * jax.nn.sigmoid(-signs * coupling_affinity_table)).astype(jnp.bfloat16)
        squashing_derivatives = lax.optimization_barrier(squashing_derivatives).astype(jnp.float32)
        picture_direction_derivative = picture_direction_derivative + affinity_multiplier * jnp.einsum('owk,okb->owb', squashing_derivatives, cycled_tiles)
        caption_share = affinity_multiplier * jnp.einsum('kox,kof->kxf', squashing_derivatives, picture_tile_sequence)
        grad_text_unit = grad_text_unit + jnp.roll(caption_share, -offset, axis=0)
    picture_direction_derivative = picture_direction_derivative.reshape(BATCH, D)
    grad_text_unit = grad_text_unit.reshape(BATCH, D)
    grad_images = (picture_direction_derivative - image_unit * lax.optimization_barrier(jnp.sum(image_unit * picture_direction_derivative, axis=1, keepdims=True))) / image_norm
    grad_texts = (grad_text_unit - text_unit * lax.optimization_barrier(jnp.sum(text_unit * grad_text_unit, axis=1, keepdims=True))) / text_norm
    loss_rows = losses.reshape(BATCH) / (WINDOW * BLOCK_ROWS)
    return (grad_images, grad_texts, loss_rows)
```

```python
import functools
import math

import jax
import jax.numpy as jnp
from jax import lax
from jax.experimental import pallas as pl
from jax.experimental.pallas import tpu as pltpu
from jax.sharding import PartitionSpec as P

EPS = 1e-06
LOG2E = math.log2(math.e)
LN2 = math.log(2.0)
AXES = ("blk", "rep")
NZ, NX = 8, 4
VMEM = pl.BlockSpec(memory_space=pltpu.VMEM)
SMEM = pl.BlockSpec(memory_space=pltpu.SMEM)


def decode(i):
    b, r = divmod(i, 4)
    z, p = divmod(b, 8)
    q, x = divmod(p, 4)
    h, c = divmod(r, 2)
    return z, q, x, h, c


def encode(z, q, x, h, c):
    return ((z % NZ) * 8 + q * 4 + (x % NX)) * 4 + h * 2 + c


def received_from(source):
    return [(encode(*source(*decode(i))), i) for i in range(NZ * 8 * 4)]


def backwards(perm):
    return [(d, s) for s, d in perm]


def flip(z, q, x, h, c):
    return z, 1 - q, x, h ^ c, c


def outer(z, q, x, h, c):
    return (z - 1 if q == 0 else z + 1), 1 - q, x, h ^ c, c


def x_shift(d):
    return received_from(lambda z, q, x, h, c: (z, q, x + d, h, c))


def in_plane_up(z, q, x, h, c):
    return (z + 1, q, x, h, c) if x == 3 else flip(z, q, x, h, c)


def in_plane_down(z, q, x, h, c):
    return (z - 1, q, x, h, c) if x == 0 else flip(z, q, x, h, c)


def in_plane_far(z, q, x, h, c):
    return (z - 1, q, x, h, c) if x <= 1 else flip(z, q, x, h, c)


def outer_far(z, q, x, h, c):
    if x <= 1:
        return (z - 1 if q == 0 else z), 1 - q, x, h ^ c, c
    return outer(z, q, x, h, c)


LEFT, RIGHT = x_shift(-1), x_shift(1)
FLIP, OUTER = received_from(flip), received_from(outer)
IN_UP, IN_DOWN, IN_FAR = (received_from(f) for f in (in_plane_up, in_plane_down, in_plane_far))
OUT_FAR = received_from(outer_far)
CORE = received_from(lambda z, q, x, h, c: (z, q, x, h, 1 - c))
HALF = received_from(lambda z, q, x, h, c: (z, q, x, 1 - h, c))


def move(value, perm):
    return lax.ppermute(value, AXES, perm)


def normalise_kernel(values, out):
    wide = values[...].astype(jnp.float32)
    norms = jnp.sqrt(jnp.sum(wide * wide, axis=1, keepdims=True) + EPS)
    out[...] = (wide / norms).astype(jnp.bfloat16)


def normalised(values):
    return pl.pallas_call(
        normalise_kernel,
        out_shape=jax.ShapeDtypeStruct(values.shape, jnp.bfloat16),
        in_specs=[VMEM],
        out_specs=VMEM,
        cost_estimate=pl.CostEstimate(
            flops=4 * values.size, bytes_accessed=4 * values.size, transcendentals=0
        ),
        name="normalise",
    )(values)


def pairs_kernel(n, own, scalars, first, images, *refs):
    texts, slopes_out, grads, loss_out = refs[:n], refs[n], refs[n + 1 : 2 * n + 1], refs[-1]
    factor, addend, scale = scalars[0], scalars[1], scalars[2]
    image = images[...]
    rows = texts[0].shape[0]
    total = None
    for k in range(n):
        cosines = lax.dot_general(
            texts[k][...], image, (((1,), (1,)), ((), ())), preferred_element_type=jnp.float32
        )
        t = cosines * factor + addend
        matched = None
        if own and k == 0:
            text_row = lax.broadcasted_iota(jnp.int32, t.shape, 0) + first[0]
            matched = text_row == lax.broadcasted_iota(jnp.int32, t.shape, 1)
            t = jnp.where(matched, -t, t)
        e = jnp.exp2(t)
        u = 1.0 + e
        r = pl.reciprocal(u, approx=True)
        slopes = e * r
        lost = (e - (u - 1.0)) * r
        q = rows // 4
        product = (u[:q] * u[q : 2 * q]) * (u[2 * q : 3 * q] * u[3 * q :])
        lost = (lost[:q] + lost[q : 2 * q]) + (lost[2 * q : 3 * q] + lost[3 * q :])
        losses = jnp.log2(product) * LN2 + lost
        losses = jnp.sum(losses.reshape(q // 8, 8, losses.shape[1]), axis=0)
        total = losses if total is None else total + losses
        if matched is not None:
            slopes = jnp.where(matched, -slopes, slopes)
        slopes = slopes.astype(jnp.bfloat16)
        slopes_out[k * rows : (k + 1) * rows, :] = slopes
        grad = jnp.dot(slopes, image, preferred_element_type=jnp.float32)
        grads[k][...] = (grad * scale).astype(jnp.bfloat16)
    loss_out[...] = total


def pairs(scalars, first, images, texts, own=False):
    n = len(texts)
    rows, width = texts[0].shape
    count = images.shape[0]
    block = jax.ShapeDtypeStruct((rows, width), jnp.bfloat16)
    out = pl.pallas_call(
        functools.partial(pairs_kernel, n, own),
        out_shape=[jax.ShapeDtypeStruct((n * rows, count), jnp.bfloat16)]
        + [block] * n
        + [jax.ShapeDtypeStruct((8, count), jnp.float32)],
        in_specs=[SMEM, SMEM] + [VMEM] * (n + 1),
        out_specs=[VMEM] * (n + 2),
        compiler_params=pltpu.CompilerParams(vmem_limit_bytes=40 << 20),
        cost_estimate=pl.CostEstimate(
            flops=4 * n * rows * count * width,
            bytes_accessed=2 * (count * width + 2 * n * rows * width + n * rows * count),
            transcendentals=2 * n * rows * count,
        ),
        name=f"pairs_{n}",
    )(scalars, first, images, *texts)
    return out[0], out[1 : n + 1], out[n + 1]


def image_kernel(counts, scalars, *refs):
    k = len(counts)
    slopes, texts, out = refs[:k], refs[k:-1], refs[-1]
    total, at = None, 0
    for part, n in zip(slopes, counts):
        block = jnp.concatenate([texts[at + j][...] for j in range(n)], axis=0)
        at += n
        share = lax.dot_general(
            part[...], block, (((0,), (0,)), ((), ())), preferred_element_type=jnp.float32
        )
        total = share if total is None else total + share
    out[...] = total * scalars[2]


def image_gradient(scalars, slopes, texts):
    counts = [s.shape[0] // texts[0].shape[0] for s in slopes]
    count, width = slopes[0].shape[1], texts[0].shape[1]
    pairs_done = sum(s.size for s in slopes)
    return pl.pallas_call(
        functools.partial(image_kernel, counts),
        out_shape=jax.ShapeDtypeStruct((count, width), jnp.float32),
        in_specs=[SMEM] + [VMEM] * (len(slopes) + len(texts)),
        out_specs=VMEM,
        compiler_params=pltpu.CompilerParams(vmem_limit_bytes=48 << 20),
        cost_estimate=pl.CostEstimate(
            flops=2 * pairs_done * width,
            bytes_accessed=2 * pairs_done + 4 * count * width + 2 * len(texts) * texts[0].size,
            transcendentals=0,
        ),
        name="image_gradient",
    )(scalars, *slopes, *texts)


def total_of(*parts):
    total = parts[0].astype(jnp.float32)
    for part in parts[1:]:
        total = total + part.astype(jnp.float32)
    return total


def summed(*parts):
    return total_of(*parts).astype(jnp.bfloat16)


def projected(grad, values):
    wide = values.astype(jnp.float32)
    norms = jnp.sqrt(jnp.sum(wide * wide, axis=1, keepdims=True) + EPS)
    unit = wide / norms
    return (grad - unit * jnp.sum(unit * grad, axis=1, keepdims=True)) / norms


def on_device(picture_vectors, caption_vectors, scale_exponent, offset_addend):
    rows, width = caption_vectors.shape
    count = picture_vectors.shape[0]
    half = rows // 2
    b, rep = lax.axis_index("blk"), lax.axis_index("rep")
    x, q, h, c = b % 4, (b // 4) % 2, rep // 2, rep % 2
    scale = jnp.exp(scale_exponent)
    scalars = jnp.concatenate([scale * LOG2E, offset_addend * LOG2E, scale])
    first = (rep * rows).astype(jnp.int32)[None]
    sends_in_left = (x == 0) & (q == 0)
    sends_in_right = (x == 3) & (q == 1)

    own = normalised(caption_vectors)
    right, left = move(own, RIGHT), move(own, LEFT)
    inner, out = move(own, FLIP), move(own, OUTER)
    images = normalised(picture_vectors)
    kernel = functools.partial(pairs, scalars, first, images)
    s0, (g_own,), l0 = kernel([own], own=True)
    far = jnp.concatenate([move(right[:half], RIGHT), move(left[half:], LEFT)])
    in_right, in_left = move(right, IN_UP), move(left, IN_DOWN)
    out_right = move(jnp.where(sends_in_left, inner, out), RIGHT)
    out_left = move(jnp.where(sends_in_right, inner, out), LEFT)
    s1, (g_right, g_left, g_inner, g_out), l1 = kernel([right, left, inner, out])
    in_far, out_far = move(far, IN_FAR), move(far, OUT_FAR)
    s2, (g_far, g_in_right, g_in_left, g_out_right, g_out_left), l2 = kernel(
        [far, in_right, in_left, out_right, out_left]
    )
    s3, (g_in_far, g_out_far), l3 = kernel([in_far, out_far])

    def back(value, perm):
        return move(value, backwards(perm))

    b_in_far, b_out_far = back(g_in_far, IN_FAR), back(g_out_far, OUT_FAR)
    b_in_right, b_in_left = back(g_in_right, IN_UP), back(g_in_left, IN_DOWN)
    b_out_right, b_out_left = back(g_out_right, RIGHT), back(g_out_left, LEFT)
    g_far = summed(g_far, b_in_far, b_out_far)
    b_far_right, b_far_left = back(g_far[:half], RIGHT), back(g_far[half:], LEFT)
    zero = jnp.zeros((), jnp.bfloat16)
    g_inner = summed(
        g_inner,
        jnp.where(sends_in_left, b_out_right, zero),
        jnp.where(sends_in_right, b_out_left, zero),
    )
    g_out = summed(
        g_out,
        jnp.where(sends_in_left, zero, b_out_right),
        jnp.where(sends_in_right, zero, b_out_left),
    )
    b_inner, b_out = back(g_inner, FLIP), back(g_out, OUTER)
    g_right = summed(g_right, b_in_right)
    g_left = summed(g_left, b_in_left)
    g_right = jnp.concatenate([summed(g_right[:half], b_far_right), g_right[half:]])
    g_left = jnp.concatenate([g_left[:half], summed(g_left[half:], b_far_left)])
    b_right, b_left = back(g_right, RIGHT), back(g_left, LEFT)
    grad_text = total_of(g_own, b_right, b_left, b_inner, b_out)
    grad_texts = projected(grad_text, caption_vectors)

    grad = image_gradient(
        scalars,
        [s0, s1, s2, s3],
        [own, right, left, inner, out, far, in_right, in_left, out_right, out_left, in_far, out_far],
    )
    losses = jnp.sum(l0 + l1 + l2 + l3, axis=0)
    grad = grad.reshape(2, 2, rows, width)
    losses = losses.reshape(2, 2, rows)

    def packed(g, l):
        g = g.reshape(-1, width).astype(jnp.bfloat16)
        l = l.reshape(-1)
        high = lax.reduce_precision(l, 8, 7)
        line = jnp.concatenate([high, l - high, jnp.zeros((width - 2 * l.size,), jnp.float32)])
        line = jnp.broadcast_to(line.astype(jnp.bfloat16), (16, width))
        return jnp.concatenate([g, line])

    def unpacked(sent, n):
        line = sent[n].astype(jnp.float32)
        return sent[:n].astype(jnp.float32), line[:n] + line[n : 2 * n]

    def pick(array, index, axis):
        return lax.dynamic_index_in_dim(array, index, axis, keepdims=False)

    sent = move(packed(pick(grad, 1 - c, 1), pick(losses, 1 - c, 1)), CORE)
    other, other_losses = unpacked(sent, 2 * rows)
    grad = pick(grad, c, 1) + other.reshape(2, rows, width)
    losses = pick(losses, c, 1) + other_losses.reshape(2, rows)
    sent = move(packed(pick(grad, 1 - h, 0), pick(losses, 1 - h, 0)), HALF)
    other, other_losses = unpacked(sent, rows)
    grad = pick(grad, h, 0) + other
    losses = pick(losses, h, 0) + other_losses
    mine = lax.dynamic_slice_in_dim(picture_vectors, rep * rows, rows, 0)
    grad_images = projected(grad, mine)
    return grad_images, grad_texts, losses / (12 * count)


def solution(mesh):
    in_specs = (P("blk", None), P(("blk", "rep"), None), P(), P())
    out_specs = (P(("blk", "rep"), None), P(("blk", "rep"), None), P(("blk", "rep")))
    return jax.shard_map(
        on_device, mesh=mesh, in_specs=in_specs, out_specs=out_specs, check_vma=False
    )
```

```python
import functools
import math

import jax
import jax.numpy as jnp
from jax import lax
from jax.experimental import pallas as pl
from jax.experimental.pallas import tpu as pltpu
from jax.sharding import PartitionSpec as P

EPS = 1e-06
LOG2E = math.log2(math.e)
LN2 = math.log(2.0)
AXES = ("blk", "rep")
NZ, NX = 8, 4
VMEM = pl.BlockSpec(memory_space=pltpu.VMEM)
SMEM = pl.BlockSpec(memory_space=pltpu.SMEM)
ANY = pl.BlockSpec(memory_space=pl.ANY)


def decode(i):
    b, r = divmod(i, 4)
    z, p = divmod(b, 8)
    q, x = divmod(p, 4)
    h, c = divmod(r, 2)
    return z, q, x, h, c


def encode(z, q, x, h, c):
    return ((z % NZ) * 8 + q * 4 + (x % NX)) * 4 + h * 2 + c


def received_from(source):
    return [(encode(*source(*decode(i))), i) for i in range(NZ * 8 * 4)]


def backwards(perm):
    return [(d, s) for s, d in perm]


def flip(z, q, x, h, c):
    return z, 1 - q, x, h ^ c, c


def outer(z, q, x, h, c):
    return (z - 1 if q == 0 else z + 1), 1 - q, x, h ^ c, c


def x_shift(d):
    return received_from(lambda z, q, x, h, c: (z, q, x + d, h, c))


def in_plane_up(z, q, x, h, c):
    return (z + 1, q, x, h, c) if x == 3 else flip(z, q, x, h, c)


def in_plane_down(z, q, x, h, c):
    return (z - 1, q, x, h, c) if x == 0 else flip(z, q, x, h, c)


def in_plane_far(z, q, x, h, c):
    return (z - 1, q, x, h, c) if x <= 1 else flip(z, q, x, h, c)


LEFT, RIGHT = x_shift(-1), x_shift(1)
FLIP, OUTER = received_from(flip), received_from(outer)
IN_UP, IN_DOWN, IN_FAR = (received_from(f) for f in (in_plane_up, in_plane_down, in_plane_far))
OPPOSITE = x_shift(2)
CORE = received_from(lambda z, q, x, h, c: (z, q, x, h, 1 - c))
HALF = received_from(lambda z, q, x, h, c: (z, q, x, 1 - h, c))


def move(value, perm):
    return lax.ppermute(value, AXES, perm)


def call(
    kernel, name, outs, *args, scalars=0, limit=16, in_specs=None, out_specs=None, scratch=()
):
    return pl.pallas_call(
        kernel,
        out_shape=[jax.ShapeDtypeStruct(out.shape, out.dtype) for out in outs],
        in_specs=in_specs or [SMEM] * scalars + [VMEM] * (len(args) - scalars),
        out_specs=out_specs or [VMEM] * len(outs),
        scratch_shapes=list(scratch),
        compiler_params=pltpu.CompilerParams(vmem_limit_bytes=limit << 20),
        cost_estimate=pl.CostEstimate(flops=1, bytes_accessed=1, transcendentals=0),
        name=name,
    )(*args)


def shaped(*shape, dtype=jnp.bfloat16):
    return jax.ShapeDtypeStruct(shape, dtype)


def inverse_norms(wide):
    return 1.0 / jnp.sqrt(jnp.sum(wide * wide, axis=1, keepdims=True) + EPS)


def normalise_kernel(values, out):
    rows = values.shape[0]
    step = min(rows, 192)
    for at in range(0, rows, step):
        wide = values[at : at + step, :].astype(jnp.float32)
        out[at : at + step, :] = (wide * inverse_norms(wide)).astype(jnp.bfloat16)


def normalised(values):
    return call(normalise_kernel, "normalise", [shaped(*values.shape)], values)[0]


def pairs_kernel(n, own, before, images_too, scalars, first, images, *refs):
    texts, refs = refs[:n], refs[n:]
    if before:
        loss_in, refs = refs[0], refs[1:]
        if images_too:
            total_in, refs = refs[0], refs[1:]
    grads, loss_out, last = refs[:n], refs[n], refs[n + 1]
    factor, addend, scale = scalars[0], scalars[1], scalars[2]
    image = images[...]
    rows = texts[0].shape[0]
    total = loss_in[...] if before else None
    parts = []
    for k in range(n):
        cosines = lax.dot_general(
            texts[k][...], image, (((1,), (1,)), ((), ())), preferred_element_type=jnp.float32
        )
        t = cosines * factor + addend
        matched = None
        if own and k == 0:
            text_row = lax.broadcasted_iota(jnp.int32, t.shape, 0) + first[0]
            matched = text_row == lax.broadcasted_iota(jnp.int32, t.shape, 1)
            t = jnp.where(matched, -t, t)
        e = jnp.exp2(t)
        u = 1.0 + e
        r = pl.reciprocal(u, approx=True)
        slopes = e * r
        lost = (e - (u - 1.0)) * r
        q = rows // 4
        product = (u[:q] * u[q : 2 * q]) * (u[2 * q : 3 * q] * u[3 * q :])
        lost = (lost[:q] + lost[q : 2 * q]) + (lost[2 * q : 3 * q] + lost[3 * q :])
        losses = jnp.log2(product) * LN2 + lost
        losses = jnp.sum(losses.reshape(q // 8, 8, losses.shape[1]), axis=0)
        total = losses if total is None else total + losses
        if matched is not None:
            slopes = jnp.where(matched, -slopes, slopes)
        slopes = slopes.astype(jnp.bfloat16)
        parts.append(slopes)
        grad = jnp.dot(slopes, image, preferred_element_type=jnp.float32)
        grads[k][...] = (grad * scale).astype(jnp.bfloat16)
    loss_out[...] = total
    slopes = jnp.concatenate(parts, axis=0)
    if not images_too:
        last[...] = slopes
        return
    share = image_share(slopes, texts)
    last[...] = total_in[...] + share if before else share


def image_share(slopes, texts):
    block = jnp.concatenate([text[...] for text in texts], axis=0)
    return lax.dot_general(
        slopes, block, (((0,), (0,)), ((), ())), preferred_element_type=jnp.float32
    )


def pairs(scalars, first, images, texts, before=(), own=False, images_too=True):
    n = len(texts)
    rows, width = texts[0].shape
    count = images.shape[0]
    outs = [shaped(rows, width)] * n + [shaped(8, count, dtype=jnp.float32)]
    if images_too:
        outs.append(shaped(count, width, dtype=jnp.float32))
    else:
        outs.append(shaped(n * rows, count))
    out = call(
        functools.partial(pairs_kernel, n, own, bool(before), images_too), f"pairs_{n}", outs,
        scalars, first, images, *texts, *before, scalars=2,
    )
    return out[:n], tuple(out[n:])


def choose(flag, first, second, out, at):
    @pl.when(flag == 1)
    def _():
        out[at:] = first[...]

    @pl.when(flag == 0)
    def _():
        out[at:] = second[...]


def pack_kernel(flags, _, right, left, inner, outer, to_left, to_right):
    half = right.shape[0] // 2
    to_left[:half] = right[:half]
    to_right[:half] = left[half:]
    choose(flags[0], inner, outer, to_left, half)
    choose(flags[1], inner, outer, to_right, half)


def unpack_kernel(flags, _, from_right, from_left, inner, outer, far, to_far):
    half = far.shape[0] // 2
    far[:half] = from_right[:half]
    far[half:] = from_left[:half]
    choose(flags[2], inner, outer, to_far, 0)


def fetch(pairs_of_refs, sems):
    copies = [pltpu.make_async_copy(*pair, sems.at[k]) for k, pair in enumerate(pairs_of_refs)]
    for copy in copies:
        copy.start()
    return copies


def merge_far_kernel(_, b_far, far, out_right, out_left, *refs):
    to_right, to_left, held, sems = refs[-4:]
    half = b_far.shape[0] // 2
    rest = pl.ds(half, out_right.shape[0])
    copies = fetch(
        [(far, held), (out_right, to_right.at[rest]), (out_left, to_left.at[rest])], sems
    )
    copies[0].wait()
    to_right[:half] = summed(held[:half], b_far[:half])
    to_left[:half] = summed(held[half:], b_far[half:])
    for copy in copies[1:]:
        copy.wait()


def merge_middle_kernel(flags, b_up, b_down, b_opposite, right, left, inner, outer, *refs):
    g_right, g_left, g_inner, g_outer, held, sems = refs[-6:]
    refs = (right, left, inner, outer)
    copies = fetch([(ref, held.at[k]) for k, ref in enumerate(refs)], sems)
    share = b_opposite[...].astype(jnp.float32)
    part = share * flags[2].astype(jnp.float32)
    for copy in copies:
        copy.wait()
    g_right[...] = summed(held[0], b_up[...])
    g_left[...] = summed(held[1], b_down[...])
    g_inner[...] = (held[2].astype(jnp.float32) + part).astype(jnp.bfloat16)
    g_outer[...] = (held[3].astype(jnp.float32) + (share - part)).astype(jnp.bfloat16)


def merge_near_kernel(flags, right, left, inner, outer, b_right, b_left, *outs):
    half = right.shape[0] // 2
    to_right, to_left, to_inner, to_outer = outs
    to_right[:half] = summed(right[:half], b_right[:half])
    to_right[half:] = right[half:]
    to_left[:half] = left[:half]
    to_left[half:] = summed(left[half:], b_left[:half])
    up = b_right[half:].astype(jnp.float32)
    down = b_left[half:].astype(jnp.float32)
    part = up * flags[0].astype(jnp.float32) + down * flags[1].astype(jnp.float32)
    to_inner[...] = (inner[...].astype(jnp.float32) + part).astype(jnp.bfloat16)
    to_outer[...] = (outer[...].astype(jnp.float32) + (up + down - part)).astype(jnp.bfloat16)


def write_losses(losses, out, at):
    count, width = losses.shape[1], out.shape[1]
    high = losses.astype(jnp.bfloat16).astype(jnp.float32)
    row = lax.broadcasted_iota(jnp.int32, (16, count), 0)
    lines = jnp.where(row == 0, high, jnp.where(row == 1, losses - high, 0.0))
    out[at : at + 16, :count] = lines.astype(jnp.bfloat16)
    out[at : at + 16, count:] = jnp.zeros((16, width - count), jnp.bfloat16)


def read_losses(ref, at, count):
    return jnp.sum(ref[at : at + 16, :count].astype(jnp.float32), axis=0, keepdims=True)


def image_kernel(n, scalars, slopes, more_slopes, loss, before, *refs):
    texts, (out, loss_out) = refs[:n], refs[n:]
    all_slopes = jnp.concatenate([slopes[...], more_slopes[...]], axis=0)
    out[...] = (before[...] + image_share(all_slopes, texts)) * scalars[2]
    loss_out[...] = jnp.sum(loss[...], axis=0, keepdims=True)


def split_kernel(place, total, loss, _, sent):
    rows = (sent.shape[0] - 16) // 2
    for j in range(2):
        start = (1 - place[1] + 2 * j) * rows
        gone = total[pl.ds(pl.multiple_of(start, rows), rows), :]
        sent[j * rows : (j + 1) * rows, :] = gone.astype(jnp.bfloat16)
    write_losses(loss[...], sent, 2 * rows)


def half_kernel(place, total, received, loss, mine, sent, loss_out):
    rows = mine.shape[0]

    def summed_core(h):
        kept = total[pl.ds(pl.multiple_of((2 * h + place[1]) * rows, rows), rows), :]
        return kept + received[pl.ds(pl.multiple_of(h * rows, rows), rows), :].astype(jnp.float32)

    mine[...] = summed_core(place[0])
    sent[:rows] = summed_core(1 - place[0]).astype(jnp.bfloat16)
    both = loss[...] + read_losses(received, 2 * rows, loss.shape[1])
    loss_out[...] = both
    write_losses(both, sent, rows)


def loss_kernel(loss, received, _, out):
    out[...] = loss[...] + read_losses(received, received.shape[0] - 16, loss.shape[1])


def last_kernel(n, values, kept, *refs):
    grads, (out, kept_held, held, sems) = refs[:n], refs[-4:]
    rows = values.shape[0]
    half = rows // 2
    (copy,) = fetch([(kept, kept_held)], sems)
    copy.wait()
    copies = []
    for j in range(2):
        here = slice(j * half, (j + 1) * half)
        wide = values[here, :].astype(jnp.float32)
        inverse = inverse_norms(wide)
        unit = wide * inverse
        grad = total_of(kept_held[here, :], *[g[here, :] for g in grads])
        along = jnp.sum(unit * grad, axis=1, keepdims=True)
        held[here, :] = (grad - unit * along) * inverse
        window = pl.ds(j * half, half)
        copies.append(
            pltpu.make_async_copy(held.at[window], out.at[window], sems.at[1 + j])
        )
        copies[-1].start()
    for copy in copies:
        copy.wait()


def projected(values, kept, *grads, after=()):
    rows, width = values.shape
    return call(
        functools.partial(last_kernel, len(grads)), "project",
        [shaped(rows, width, dtype=jnp.float32)],
        values, kept, *grads, *after,
        in_specs=[VMEM, ANY] + [VMEM] * len(grads) + [ANY] * len(after),
        out_specs=[ANY],
        scratch=[
            pltpu.VMEM((rows, width), kept.dtype),
            pltpu.VMEM((rows, width), jnp.float32),
            pltpu.SemaphoreType.DMA((3,)),
        ],
    )[0]


def total_of(*parts):
    total = parts[0].astype(jnp.float32)
    for part in parts[1:]:
        total = total + part.astype(jnp.float32)
    return total


def summed(*parts):
    return total_of(*parts).astype(jnp.bfloat16)


def on_device(picture_vectors, caption_vectors, scale_exponent, offset_addend):
    rows, width = caption_vectors.shape
    count = picture_vectors.shape[0]
    half = rows // 2
    b, rep = lax.axis_index("blk"), lax.axis_index("rep")
    x, q, h, c = b % 4, (b // 4) % 2, rep // 2, rep % 2
    scale = jnp.exp(scale_exponent)
    scalars = jnp.concatenate([scale * LOG2E, offset_addend * LOG2E, scale])
    first = (rep * rows).astype(jnp.int32)[None]
    place = jnp.stack([h, c]).astype(jnp.int32)
    flags = jnp.stack([(x == 0) & (q == 0), (x == 3) & (q == 1), (x >= 2) & (q == 1)])
    flags = flags.astype(jnp.int32)
    kernel = functools.partial(pairs, scalars, first)

    own = normalised(caption_vectors)
    right, left = move(own, RIGHT), move(own, LEFT)
    inner, outer = move(own, FLIP), move(own, OUTER)
    images = normalised(picture_vectors)
    (g_own,), sums = kernel(images, [own], own=True)
    packet = shaped(rows + half, width)
    to_left, to_right = call(
        pack_kernel, "pack", [packet, packet],
        flags, sums[0], right, left, inner, outer, scalars=1,
    )
    from_right, from_left = move(to_left, RIGHT), move(to_right, LEFT)
    up, down = move(right, IN_UP), move(left, IN_DOWN)
    (g_right, g_left, g_inner, g_outer), sums = kernel(images, [right, left, inner, outer], sums)
    far, to_far = call(
        unpack_kernel, "unpack", [shaped(rows, width)] * 2,
        flags, sums[0], from_right, from_left, inner, outer, scalars=1,
    )
    out_right, out_left = from_right[half:], from_left[half:]
    far_inner, far_outer = move(far, IN_FAR), move(to_far, OPPOSITE)
    (g_far, g_up, g_down, g_out_right, g_out_left), sums = kernel(
        images, [far, up, down, out_right, out_left], sums
    )
    loss, total = sums
    (g_far_inner,), (loss, slopes) = kernel(images, [far_inner], (loss,), images_too=False)
    (g_far_outer,), (loss, more_slopes) = kernel(images, [far_outer], (loss,), images_too=False)

    def back(value, perm):
        return move(value, backwards(perm))

    b_far_inner, b_far_outer = back(g_far_inner, IN_FAR), back(g_far_outer, OPPOSITE)
    b_up, b_down = back(g_up, IN_UP), back(g_down, IN_DOWN)
    total, loss = call(
        functools.partial(image_kernel, 2), "image_gradient",
        [shaped(count, width, dtype=jnp.float32), shaped(1, count, dtype=jnp.float32)],
        scalars, slopes, more_slopes, loss, total, far_inner, far_outer, scalars=1,
    )
    wide = shaped(rows, width, dtype=jnp.float32)
    block = shaped(rows, width)
    to_right, to_left = call(
        merge_far_kernel, "merge_far", [packet, packet],
        loss, b_far_inner, g_far, g_out_right, g_out_left, b_up, b_down, b_far_outer,
        in_specs=[VMEM] * 2 + [ANY] * 6,
        scratch=[pltpu.VMEM((rows, width), jnp.bfloat16), pltpu.SemaphoreType.DMA((3,))],
    )
    g_right, g_left, g_inner, g_outer = call(
        merge_middle_kernel, "merge_middle", [block] * 4,
        flags, b_up, b_down, b_far_outer, g_right, g_left, g_inner, g_outer, to_right,
        in_specs=[SMEM] + [VMEM] * 3 + [ANY] * 5,
        scratch=[pltpu.VMEM((4, rows, width), jnp.bfloat16), pltpu.SemaphoreType.DMA((4,))],
    )
    b_right, b_left = back(to_right, RIGHT), back(to_left, LEFT)
    (sent,) = call(
        split_kernel, "split", [shaped(2 * rows + 16, width)], place, total, loss, to_right, scalars=1
    )
    received = move(sent, CORE)
    mine, sent, loss = call(
        half_kernel, "half", [wide, shaped(rows + 16, width), loss],
        place, total, received, loss, scalars=1,
    )
    received = move(sent, HALF)
    g_right, g_left, g_inner, g_outer = call(
        merge_near_kernel, "merge_near", [shaped(rows, width)] * 4,
        flags, g_right, g_left, g_inner, g_outer, b_right, b_left, scalars=1,
    )
    b_right, b_left = back(g_right, RIGHT), back(g_left, LEFT)
    b_inner, b_outer = back(g_inner, FLIP), back(g_outer, OUTER)
    pictures = lax.dynamic_slice_in_dim(picture_vectors, rep * rows, rows, 0)
    grad_images = projected(pictures, mine, received[:rows])
    (loss,) = call(
        loss_kernel, "losses", [loss], loss, received, grad_images, in_specs=[VMEM, VMEM, ANY]
    )
    loss_rows = lax.dynamic_slice_in_dim(loss[0], rep * rows, rows, 0) / (12 * count)
    grad_texts = projected(
        caption_vectors, g_own, b_right, b_left, b_inner, b_outer, after=(loss,)
    )
    return grad_images, grad_texts, loss_rows


def solution(mesh):
    in_specs = (P("blk", None), P(("blk", "rep"), None), P(), P())
    out_specs = (P(("blk", "rep"), None), P(("blk", "rep"), None), P(("blk", "rep")))
    return jax.shard_map(
        on_device, mesh=mesh, in_specs=in_specs, out_specs=out_specs, check_vma=False
    )
```

```python
import functools
import math

import jax
import jax.numpy as jnp
from jax import lax
from jax.experimental import pallas as pl
from jax.experimental.pallas import tpu as pltpu
from jax.sharding import PartitionSpec as P

EPS = 1e-06
LOG2E = math.log2(math.e)
LN2 = math.log(2.0)
AXES = ("blk", "rep")
NZ, NX = 8, 4
VMEM = pl.BlockSpec(memory_space=pltpu.VMEM)
SMEM = pl.BlockSpec(memory_space=pltpu.SMEM)
ANY = pl.BlockSpec(memory_space=pl.ANY)


def decode(i):
    b, r = divmod(i, 4)
    z, p = divmod(b, 8)
    q, x = divmod(p, 4)
    h, c = divmod(r, 2)
    return z, q, x, h, c


def encode(z, q, x, h, c):
    return ((z % NZ) * 8 + q * 4 + (x % NX)) * 4 + h * 2 + c


def received_from(source):
    return [(encode(*source(*decode(i))), i) for i in range(NZ * 8 * 4)]


def backwards(perm):
    return [(d, s) for s, d in perm]


def flip(z, q, x, h, c):
    return z, 1 - q, x, h ^ c, c


def outer(z, q, x, h, c):
    return (z - 1 if q == 0 else z + 1), 1 - q, x, h ^ c, c


def x_shift(d):
    return received_from(lambda z, q, x, h, c: (z, q, x + d, h, c))


def in_plane_up(z, q, x, h, c):
    return (z + 1, q, x, h, c) if x == 3 else flip(z, q, x, h, c)


def in_plane_down(z, q, x, h, c):
    return (z - 1, q, x, h, c) if x == 0 else flip(z, q, x, h, c)


def in_plane_far(z, q, x, h, c):
    return (z - 1, q, x, h, c) if x <= 1 else flip(z, q, x, h, c)


LEFT, RIGHT = x_shift(-1), x_shift(1)
FLIP, OUTER = received_from(flip), received_from(outer)
IN_UP, IN_DOWN, IN_FAR = (received_from(f) for f in (in_plane_up, in_plane_down, in_plane_far))
OPPOSITE = x_shift(2)
CORE = received_from(lambda z, q, x, h, c: (z, q, x, h, 1 - c))
HALF = received_from(lambda z, q, x, h, c: (z, q, x, 1 - h, c))


def move(value, perm):
    return lax.ppermute(value, AXES, perm)


def call(
    kernel, name, outs, *args,
    scalars=0, limit=16, in_specs=None, out_specs=None, scratch=(), flops=1,
):
    return pl.pallas_call(
        kernel,
        out_shape=[jax.ShapeDtypeStruct(out.shape, out.dtype) for out in outs],
        in_specs=in_specs or [SMEM] * scalars + [VMEM] * (len(args) - scalars),
        out_specs=out_specs or [VMEM] * len(outs),
        scratch_shapes=list(scratch),
        compiler_params=pltpu.CompilerParams(vmem_limit_bytes=limit << 20),
        cost_estimate=pl.CostEstimate(flops=flops, bytes_accessed=1, transcendentals=0),
        name=name,
    )(*args)


def shaped(*shape, dtype=jnp.bfloat16):
    return jax.ShapeDtypeStruct(shape, dtype)


def inverse_norms(wide):
    return 1.0 / jnp.sqrt(jnp.sum(wide * wide, axis=1, keepdims=True) + EPS)


def normalise_kernel(values, out):
    rows = values.shape[0]
    step = min(rows, 192)
    for at in range(0, rows, step):
        wide = values[at : at + step, :].astype(jnp.float32)
        out[at : at + step, :] = (wide * inverse_norms(wide)).astype(jnp.bfloat16)


def normalised(values):
    return call(normalise_kernel, "normalise", [shaped(*values.shape)], values)[0]


def last_rows(ref, rows):
    return ref[ref.shape[0] - rows :, :]


def image_share(slopes, texts, rows):
    block = jnp.concatenate([last_rows(text, rows) for text in texts], axis=0)
    return lax.dot_general(
        slopes, block, (((0,), (0,)), ((), ())), preferred_element_type=jnp.float32
    )


def pairs_kernel(n, rows, own, joined, sums, scalars, first, images, *refs):
    texts, last = refs[:n], refs[-1]
    grads = refs[-2:-1] if joined else refs[-n - 1 : -1]
    factor, addend, scale = scalars[0], scalars[1], scalars[2]
    image = images[...]
    count = image.shape[0]
    total = None
    parts = []
    for k in range(n):
        cosines = lax.dot_general(
            last_rows(texts[k], rows), image, (((1,), (1,)), ((), ())),
            preferred_element_type=jnp.float32,
        )
        t = cosines * factor + addend
        matched = None
        if own and k == 0:
            text_row = lax.broadcasted_iota(jnp.int32, t.shape, 0) + first[0]
            matched = text_row == lax.broadcasted_iota(jnp.int32, t.shape, 1)
            t = jnp.where(matched, -t, t)
        e = jnp.exp2(t)
        u = 1.0 + e
        r = pl.reciprocal(u, approx=True)
        slopes = e * r
        lost = (e - (u - 1.0)) * r
        q = rows // 4
        product = (u[:q] * u[q : 2 * q]) * (u[2 * q : 3 * q] * u[3 * q :])
        lost = (lost[:q] + lost[q : 2 * q]) + (lost[2 * q : 3 * q] + lost[3 * q :])
        losses = jnp.log2(product) * LN2 + lost
        losses = jnp.sum(losses.reshape(q // 8, 8, losses.shape[1]), axis=0)
        total = losses if total is None else total + losses
        if matched is not None:
            slopes = jnp.where(matched, -slopes, slopes)
        slopes = slopes.astype(jnp.bfloat16)
        if sums == 0:
            last[k * rows : (k + 1) * rows, :] = slopes
        else:
            parts.append(slopes)
        grad = jnp.dot(slopes, image, preferred_element_type=jnp.float32)
        grad = (grad * scale).astype(jnp.bfloat16)
        if joined:
            grads[0][k * rows : (k + 1) * rows, :] = grad
        else:
            grads[k][...] = grad
    if sums == 0:
        high = total.astype(jnp.bfloat16)
        low = (total - high.astype(jnp.float32)).astype(jnp.bfloat16)
        last[n * rows :, :] = jnp.concatenate([high, low], axis=0)
        return
    share = image_share(jnp.concatenate(parts, axis=0), texts, rows)
    before = refs[n] if sums == 2 else None
    last[:count, :] = before[:count, :] + share if sums == 2 else share
    last[count:, :count] = before[count:, :count] + total if sums == 2 else total


def pairs(scalars, first, rows, images, texts, after=(), own=False, joined=False, sums=0, before=()):
    n, width = len(texts), images.shape[1]
    count = images.shape[0]
    outs = [shaped(n * rows, width)] if joined else [shaped(rows, width)] * n
    if sums:
        outs.append(shaped(count + 8, width, dtype=jnp.float32))
    else:
        outs.append(shaped(n * rows + 16, count))
    out = call(
        functools.partial(pairs_kernel, n, rows, own, joined, sums), f"pairs_{n}", outs,
        scalars, first, images, *texts, *before, *after,
        in_specs=[SMEM] * 2 + [VMEM] * (1 + n + len(before)) + [ANY] * len(after),
    )
    return out[:-1], out[-1]


def choose(flag, first, second, out, at):
    @pl.when(flag == 1)
    def _():
        out[at:] = first[...]

    @pl.when(flag == 0)
    def _():
        out[at:] = second[...]


def pack_kernel(flags, _, right, left, inner, outer, to_left, to_right):
    half = right.shape[0] // 2
    to_left[:half] = right[:half]
    to_right[:half] = left[half:]
    choose(flags[0], inner, outer, to_left, half)
    choose(flags[1], inner, outer, to_right, half)


def unpack_kernel(flags, _, from_right, from_left, inner, outer, far, to_far):
    half = far.shape[0] // 2
    far[:half] = from_right[:half]
    far[half:] = from_left[:half]
    choose(flags[2], inner, outer, to_far, 0)


def fetch(pairs_of_refs, sems):
    copies = [pltpu.make_async_copy(*pair, sems.at[k]) for k, pair in enumerate(pairs_of_refs)]
    for copy in copies:
        copy.start()
    return copies


def merge_far_kernel(b_far, far, *refs):
    to_right, to_left, held, sems = refs[-4:]
    half = b_far.shape[0] // 2
    (copy,) = fetch([(far, held)], sems)
    copy.wait()
    to_right[...] = summed(held[:half], b_far[:half])
    to_left[...] = summed(held[half:], b_far[half:])


def merge_sides_kernel(b_up, b_down, grads, _, g_right, g_left, held, sems):
    rows = b_up.shape[0]
    (copy,) = fetch([(grads.at[pl.ds(0, 2 * rows)], held)], sems)
    copy.wait()
    g_right[...] = summed(held[:rows], b_up[...])
    g_left[...] = summed(held[rows:], b_down[...])


def merge_column_kernel(flags, b_right, b_left, b_opposite, grads, _, to_inner, to_outer, held, sems):
    rows = b_right.shape[0]
    (copy,) = fetch([(grads.at[pl.ds(2 * rows, 2 * rows)], held)], sems)
    shares = [ref[...].astype(jnp.float32) for ref in (b_right, b_left, b_opposite)]
    weights = [flags[k].astype(jnp.float32) for k in range(3)]
    part = shares[0] * weights[0] + shares[1] * weights[1] + shares[2] * weights[2]
    rest = (shares[0] + shares[1]) + (shares[2] - part)
    copy.wait()
    to_inner[...] = (held[:rows].astype(jnp.float32) + part).astype(jnp.bfloat16)
    to_outer[...] = (held[rows:].astype(jnp.float32) + rest).astype(jnp.bfloat16)


def merge_near_kernel(right, left, b_right, b_left, to_right, to_left):
    half = right.shape[0] // 2
    to_right[:half] = summed(right[:half], b_right[...])
    to_right[half:] = right[half:]
    to_left[:half] = left[:half]
    to_left[half:] = summed(left[half:], b_left[...])


def write_losses(losses, out, at):
    count, width = losses.shape[1], out.shape[1]
    high = losses.astype(jnp.bfloat16).astype(jnp.float32)
    row = lax.broadcasted_iota(jnp.int32, (16, count), 0)
    lines = jnp.where(row == 0, high, jnp.where(row == 1, losses - high, 0.0))
    out[at : at + 16, :count] = lines.astype(jnp.bfloat16)
    if width > count:
        out[at : at + 16, count:] = jnp.zeros((16, width - count), jnp.bfloat16)


def read_losses(ref, at, count):
    return jnp.sum(ref[at : at + 16, :count].astype(jnp.float32), axis=0, keepdims=True)


def image_kernel(counts, place, scalars, before, *refs):
    k, n = len(counts), sum(counts)
    slopes, texts, refs = refs[:k], refs[k : k + n], refs[k + n :]
    sent, kept, before_held, slopes_held, texts_held, sems = refs
    rows, count = texts_held.shape[0] // n, slopes_held.shape[1]
    groups, used, at, first = [], 0, 0, 0
    for s, m in zip(slopes, counts):
        moves = [(s, slopes_held.at[pl.ds(at, m * rows + 16)])]
        for j in range(first, first + m):
            block = texts[j].at[pl.ds(texts[j].shape[0] - rows, rows)]
            moves.append((block, texts_held.at[pl.ds(j * rows, rows)]))
        at += m * rows + 16
        first += m
        groups.append((moves, used))
        used += len(moves)
    groups.append(([(before, before_held)], used))
    groups = [
        [pltpu.make_async_copy(*pair, sems.at[base + i]) for i, pair in enumerate(moves)]
        for moves, base in groups
    ]
    for group in groups:
        for copy in group:
            copy.start()
    total, at, first, lines = None, 0, 0, []
    middle = k // 2
    for part in ((0, middle), (middle, k)):
        for group in groups[part[0] : part[1]]:
            for copy in group:
                copy.wait()
        every, start = [], first
        for m in counts[part[0] : part[1]]:
            every.append(slopes_held[at : at + m * rows, :])
            lines.append(at + m * rows)
            at += m * rows + 16
            first += m
        share = lax.dot_general(
            jnp.concatenate(every, axis=0), texts_held[start * rows : first * rows, :],
            (((0,), (0,)), ((), ())), preferred_element_type=jnp.float32,
        )
        total = share if total is None else total + share
    groups[-1][0].wait()
    before_held[:count, :] = (before_held[:count, :] + total) * scalars[2]
    loss = before_held[count:, :count]
    for line in lines:
        both = slopes_held[line : line + 16, :].astype(jnp.float32)
        loss = loss + (both[:8] + both[8:])
    loss = jnp.sum(loss, axis=0, keepdims=True)
    for j in range(2):
        here = slice(j * rows, (j + 1) * rows)
        mine, other = ((c + 2 * j) * rows for c in (place[1], 1 - place[1]))
        kept[here, :] = before_held[pl.ds(pl.multiple_of(mine, rows), rows), :]
        gone = before_held[pl.ds(pl.multiple_of(other, rows), rows), :]
        sent[here, :] = gone.astype(jnp.bfloat16)
    write_losses(loss, sent, 2 * rows)
    kept[2 * rows :, :count] = jnp.broadcast_to(loss, (8, count))


def image_gradient(place, scalars, rows, before, slopes, texts):
    width = texts[0].shape[1]
    count = slopes[0].shape[1]
    counts = [(s.shape[0] - 16) // rows for s in slopes]
    return call(
        functools.partial(image_kernel, counts), "image_gradient",
        [shaped(2 * rows + 16, width), shaped(2 * rows + 8, width, dtype=jnp.float32)],
        place, scalars, before, *slopes, *texts,
        limit=56,
        in_specs=[SMEM] * 2 + [ANY] * (1 + len(slopes) + len(texts)),
        scratch=[
            pltpu.VMEM((count + 8, width), jnp.float32),
            pltpu.VMEM((sum(s.shape[0] for s in slopes), count), jnp.bfloat16),
            pltpu.VMEM((len(texts) * rows, width), jnp.bfloat16),
            pltpu.SemaphoreType.DMA((1 + len(slopes) + len(texts),)),
        ],
    )


def half_kernel(place, kept, received, _, mine, sent, loss_out):
    rows, count = mine.shape[0], loss_out.shape[1]

    def summed_core(h):
        here = pl.ds(pl.multiple_of(h * rows, rows), rows)
        return kept[here, :] + received[here, :].astype(jnp.float32)

    mine[...] = summed_core(place[0])
    sent[:rows] = summed_core(1 - place[0]).astype(jnp.bfloat16)
    both = kept[2 * rows : 2 * rows + 1, :count] + read_losses(received, 2 * rows, count)
    loss_out[...] = both
    write_losses(both, sent, rows)


def loss_kernel(loss, received, _, out):
    out[...] = loss[...] + read_losses(received, received.shape[0] - 16, loss.shape[1])


def last_kernel(n, values, kept, *refs):
    grads, (out, kept_held, held, sems) = refs[:n], refs[-4:]
    rows = values.shape[0]
    half = rows // 4
    (copy,) = fetch([(kept, kept_held)], sems)
    inverses = inverse_norms(values[...].astype(jnp.float32))
    copy.wait()
    copies = []
    for j in range(4):
        here = slice(j * half, (j + 1) * half)
        wide = values[here, :].astype(jnp.float32)
        inverse = inverses[here, :]
        unit = wide * inverse
        grad = total_of(kept_held[here, :], *[g[here, :] for g in grads])
        along = jnp.sum(unit * grad, axis=1, keepdims=True)
        held[here, :] = (grad - unit * along) * inverse
        window = pl.ds(j * half, half)
        copies.append(
            pltpu.make_async_copy(held.at[window], out.at[window], sems.at[1 + j])
        )
        copies[-1].start()
    for copy in copies:
        copy.wait()


def projected(values, kept, *grads, after=()):
    rows, width = values.shape
    return call(
        functools.partial(last_kernel, len(grads)), "project",
        [shaped(rows, width, dtype=jnp.float32)],
        values, kept, *grads, *after,
        in_specs=[VMEM, ANY] + [VMEM] * len(grads) + [ANY] * len(after),
        out_specs=[ANY],
        scratch=[
            pltpu.VMEM((rows, width), kept.dtype),
            pltpu.VMEM((rows, width), jnp.float32),
            pltpu.SemaphoreType.DMA((5,)),
        ],
    )[0]


def total_of(*parts):
    total = parts[0].astype(jnp.float32)
    for part in parts[1:]:
        total = total + part.astype(jnp.float32)
    return total


def summed(*parts):
    return total_of(*parts).astype(jnp.bfloat16)


def on_device(picture_vectors, caption_vectors, scale_exponent, offset_addend):
    rows, width = caption_vectors.shape
    count = picture_vectors.shape[0]
    half = rows // 2
    b, rep = lax.axis_index("blk"), lax.axis_index("rep")
    x, q, h, c = b % 4, (b // 4) % 2, rep // 2, rep % 2
    scale = jnp.exp(scale_exponent)
    scalars = jnp.concatenate([scale * LOG2E, offset_addend * LOG2E, scale])
    first = (rep * rows).astype(jnp.int32)[None]
    place = jnp.stack([h, c]).astype(jnp.int32)
    flags = jnp.stack([(x == 0) & (q == 0), (x == 3) & (q == 1), (x >= 2) & (q == 1)])
    flags = flags.astype(jnp.int32)
    kernel = functools.partial(pairs, scalars, first, rows)

    own = normalised(caption_vectors)
    right, left = move(own, RIGHT), move(own, LEFT)
    inner, outer = move(own, FLIP), move(own, OUTER)
    images = normalised(picture_vectors)
    block, piece = shaped(rows, width), shaped(half, width)
    packet = shaped(rows + half, width)
    (g_own,), total = kernel(images, [own], own=True, sums=1)
    to_left, to_right = call(
        pack_kernel, "pack", [packet, packet], flags, g_own, right, left, inner, outer,
        in_specs=[SMEM, ANY] + [VMEM] * 4,
    )
    from_right, from_left = move(to_left, RIGHT), move(to_right, LEFT)
    up, down = move(right, IN_UP), move(left, IN_DOWN)
    (g_near,), total = kernel(
        images, [right, left, inner, outer], joined=True, sums=2, before=(total,)
    )
    far, to_far = call(
        unpack_kernel, "unpack", [block] * 2,
        flags, g_near, from_right, from_left, inner, outer,
        in_specs=[SMEM, ANY] + [VMEM] * 4,
    )
    far_inner, far_outer = move(far, IN_FAR), move(to_far, OPPOSITE)
    (g_up, g_down), s_sides = kernel(images, [up, down])
    (g_far, g_out_right, g_out_left), s_near = kernel(
        images, [far, from_right, from_left], after=(s_sides,)
    )
    (g_far_inner, g_far_outer), s_far = kernel(
        images, [far_inner, far_outer], after=(s_near,)
    )

    def back(value, perm):
        return move(value, backwards(perm))

    b_up, b_down = back(g_up, IN_UP), back(g_down, IN_DOWN)
    b_out_right, b_out_left = back(g_out_right, RIGHT), back(g_out_left, LEFT)
    b_far_inner, b_far_outer = back(g_far_inner, IN_FAR), back(g_far_outer, OPPOSITE)
    held = [pltpu.VMEM((2 * rows, width), jnp.bfloat16), pltpu.SemaphoreType.DMA((1,))]
    g_right, g_left = call(
        merge_sides_kernel, "merge_sides", [block] * 2, b_up, b_down, g_near, s_far,
        in_specs=[VMEM] * 2 + [ANY] * 2, scratch=held,
    )
    sent, kept = image_gradient(
        place, scalars, rows, total,
        [s_sides, s_near, s_far],
        [up, down, far, from_right, from_left, far_inner, far_outer],
    )
    received = move(sent, CORE)
    wide = shaped(rows, width, dtype=jnp.float32)
    to_right, to_left = call(
        merge_far_kernel, "merge_far", [piece] * 2,
        b_far_inner, g_far, b_far_outer, b_out_right, b_out_left, sent, g_right,
        in_specs=[VMEM] + [ANY] * 6,
        scratch=[pltpu.VMEM((rows, width), jnp.bfloat16), pltpu.SemaphoreType.DMA((1,))],
        flops=20_000_000_000,
    )
    g_inner, g_outer = call(
        merge_column_kernel, "merge_column", [block] * 2,
        flags, b_out_right, b_out_left, b_far_outer, g_near, to_left,
        in_specs=[SMEM] + [VMEM] * 3 + [ANY] * 2, scratch=held,
    )
    b_right, b_left = back(to_right, RIGHT), back(to_left, LEFT)
    mine, sent, loss = call(
        half_kernel, "half", [wide, shaped(rows + 16, width), shaped(1, count, dtype=jnp.float32)],
        place, kept, received, to_left,
        in_specs=[SMEM, VMEM, VMEM, ANY],
    )
    received = move(sent, HALF)
    g_right, g_left = call(
        merge_near_kernel, "merge_near", [block] * 2, g_right, g_left, b_right, b_left
    )
    b_right, b_left = back(g_right, RIGHT), back(g_left, LEFT)
    b_inner, b_outer = back(g_inner, FLIP), back(g_outer, OUTER)
    pictures = lax.dynamic_slice_in_dim(picture_vectors, rep * rows, rows, 0)
    grad_images = projected(pictures, mine, received[:rows])
    (loss,) = call(
        loss_kernel, "losses", [loss], loss, received, grad_images, in_specs=[VMEM, VMEM, ANY]
    )
    loss_rows = lax.dynamic_slice_in_dim(loss[0], rep * rows, rows, 0) / (12 * count)
    grad_texts = projected(
        caption_vectors, g_own, b_right, b_left, b_inner, b_outer, after=(loss,)
    )
    return grad_images, grad_texts, loss_rows


def solution(mesh):
    in_specs = (P("blk", None), P(("blk", "rep"), None), P(), P())
    out_specs = (P(("blk", "rep"), None), P(("blk", "rep"), None), P(("blk", "rep")))
    return jax.shard_map(
        on_device, mesh=mesh, in_specs=in_specs, out_specs=out_specs, check_vma=False
    )
```

```python
import functools
import math

import jax
import jax.numpy as jnp
from jax import lax
from jax.experimental import pallas as pl
from jax.experimental.pallas import tpu as pltpu
from jax.sharding import PartitionSpec as P

EPS = 1e-06
LOG2E = math.log2(math.e)
LN2 = math.log(2.0)
AXES = ("blk", "rep")
NZ, NX = 8, 4
VMEM = pl.BlockSpec(memory_space=pltpu.VMEM)
SMEM = pl.BlockSpec(memory_space=pltpu.SMEM)
ANY = pl.BlockSpec(memory_space=pl.ANY)


def decode(i):
    b, r = divmod(i, 4)
    z, p = divmod(b, 8)
    q, x = divmod(p, 4)
    h, c = divmod(r, 2)
    return z, q, x, h, c


def encode(z, q, x, h, c):
    return ((z % NZ) * 8 + q * 4 + (x % NX)) * 4 + h * 2 + c


def received_from(source):
    return [(encode(*source(*decode(i))), i) for i in range(NZ * 8 * 4)]


def backwards(perm):
    return [(d, s) for s, d in perm]


def flip(z, q, x, h, c):
    return z, 1 - q, x, h ^ c, c


def outer(z, q, x, h, c):
    return (z - 1 if q == 0 else z + 1), 1 - q, x, h ^ c, c


def x_shift(d):
    return received_from(lambda z, q, x, h, c: (z, q, x + d, h, c))


def in_plane_up(z, q, x, h, c):
    return (z + 1, q, x, h, c) if x == 3 else flip(z, q, x, h, c)


def in_plane_down(z, q, x, h, c):
    return (z - 1, q, x, h, c) if x == 0 else flip(z, q, x, h, c)


def in_plane_far(z, q, x, h, c):
    return (z - 1, q, x, h, c) if x <= 1 else flip(z, q, x, h, c)


LEFT, RIGHT = x_shift(-1), x_shift(1)
FLIP, OUTER = received_from(flip), received_from(outer)
IN_UP, IN_DOWN, IN_FAR = (received_from(f) for f in (in_plane_up, in_plane_down, in_plane_far))
OPPOSITE = x_shift(2)
CORE = received_from(lambda z, q, x, h, c: (z, q, x, h, 1 - c))
HALF = received_from(lambda z, q, x, h, c: (z, q, x, 1 - h, c))


def move(value, perm):
    return lax.ppermute(value, AXES, perm)


def call(
    kernel, name, outs, *args,
    scalars=0, limit=16, in_specs=None, out_specs=None, scratch=(), flops=1,
):
    return pl.pallas_call(
        kernel,
        out_shape=[jax.ShapeDtypeStruct(out.shape, out.dtype) for out in outs],
        in_specs=in_specs or [SMEM] * scalars + [VMEM] * (len(args) - scalars),
        out_specs=out_specs or [VMEM] * len(outs),
        scratch_shapes=list(scratch),
        compiler_params=pltpu.CompilerParams(vmem_limit_bytes=limit << 20),
        cost_estimate=pl.CostEstimate(flops=flops, bytes_accessed=1, transcendentals=0),
        name=name,
    )(*args)


def shaped(*shape, dtype=jnp.bfloat16):
    return jax.ShapeDtypeStruct(shape, dtype)


def inverse_norms(wide):
    return 1.0 / jnp.sqrt(jnp.sum(wide * wide, axis=1, keepdims=True) + EPS)


def normalise_kernel(values, out):
    rows = values.shape[0]
    step = min(rows, 192)
    for at in range(0, rows, step):
        wide = values[at : at + step, :].astype(jnp.float32)
        out[at : at + step, :] = (wide * inverse_norms(wide)).astype(jnp.bfloat16)


def normalised(values):
    return call(normalise_kernel, "normalise", [shaped(*values.shape)], values)[0]


def last_rows(ref, rows):
    return ref[ref.shape[0] - rows :, :]


def pairs_kernel(n, rows, own, joined, sums, scalars, first, images, *refs):
    texts, last = refs[:n], refs[-1]
    grads = refs[-2:-1] if joined else refs[-n - 1 : -1]
    factor, addend, scale = scalars[0], scalars[1], scalars[2]
    image = images[...]
    count = image.shape[0]
    block = jnp.concatenate([last_rows(text, rows) for text in texts], axis=0)
    cosines = lax.dot_general(
        block, image, (((1,), (1,)), ((), ())), preferred_element_type=jnp.float32
    )
    t = cosines * factor + addend
    if own:
        text_row = lax.broadcasted_iota(jnp.int32, t.shape, 0) + first[0]
        matched = text_row == lax.broadcasted_iota(jnp.int32, t.shape, 1)
        t = jnp.where(matched, -t, t)
    e = jnp.exp2(t)
    u = 1.0 + e
    r = pl.reciprocal(u, approx=True)
    slopes = e * r
    lost = (e - (u - 1.0)) * r
    q = n * rows // 4
    product = (u[:q] * u[q : 2 * q]) * (u[2 * q : 3 * q] * u[3 * q :])
    lost = (lost[:q] + lost[q : 2 * q]) + (lost[2 * q : 3 * q] + lost[3 * q :])
    losses = jnp.log2(product) * LN2 + lost
    total = jnp.sum(losses.reshape(q // 8, 8, count), axis=0)
    if own:
        slopes = jnp.where(matched, -slopes, slopes)
    slopes = slopes.astype(jnp.bfloat16)
    grad = jnp.dot(slopes, image, preferred_element_type=jnp.float32)
    grad = (grad * scale).astype(jnp.bfloat16)
    if joined:
        grads[0][...] = grad
    else:
        for k in range(n):
            grads[k][...] = grad[k * rows : (k + 1) * rows]
    if sums == 0:
        last[: n * rows, :] = slopes
        high = total.astype(jnp.bfloat16)
        low = (total - high.astype(jnp.float32)).astype(jnp.bfloat16)
        last[n * rows :, :] = jnp.concatenate([high, low], axis=0)
        return
    share = lax.dot_general(
        slopes, block, (((0,), (0,)), ((), ())), preferred_element_type=jnp.float32
    )
    before = refs[n] if sums == 2 else None
    last[:count, :] = before[:count, :] + share if sums == 2 else share
    last[count:, :count] = before[count:, :count] + total if sums == 2 else total


def pairs(scalars, first, rows, images, texts, after=(), own=False, joined=False, sums=0, before=()):
    n, width = len(texts), images.shape[1]
    count = images.shape[0]
    outs = [shaped(n * rows, width)] if joined else [shaped(rows, width)] * n
    if sums:
        outs.append(shaped(count + 8, width, dtype=jnp.float32))
    else:
        outs.append(shaped(n * rows + 16, count))
    out = call(
        functools.partial(pairs_kernel, n, rows, own, joined, sums), f"pairs_{n}", outs,
        scalars, first, images, *texts, *before, *after,
        in_specs=[SMEM] * 2 + [VMEM] * (1 + n + len(before)) + [ANY] * len(after),
    )
    return out[:-1], out[-1]


def choose(flag, first, second, out, at):
    @pl.when(flag == 1)
    def _():
        out[at:] = first[...]

    @pl.when(flag == 0)
    def _():
        out[at:] = second[...]


def pack_kernel(flags, outer, _, right, left, inner, to_left, to_right):
    half = right.shape[0] // 2
    to_left[:half] = right[:half]
    to_right[:half] = left[half:]
    choose(flags[0], inner, outer, to_left, half)
    choose(flags[1], inner, outer, to_right, half)


def unpack_kernel(flags, _, from_right, from_left, inner, outer, far, to_far):
    half = far.shape[0] // 2
    far[:half] = from_right[:half]
    far[half:] = from_left[:half]
    choose(flags[2], inner, outer, to_far, 0)


def fetch(pairs_of_refs, sems):
    copies = [pltpu.make_async_copy(*pair, sems.at[k]) for k, pair in enumerate(pairs_of_refs)]
    for copy in copies:
        copy.start()
    return copies


def merge_far_kernel(b_far, far, *refs):
    to_right, to_left, held, sems = refs[-4:]
    half = b_far.shape[0] // 2
    (copy,) = fetch([(far, held)], sems)
    copy.wait()
    to_right[...] = summed(held[:half], b_far[:half])
    to_left[...] = summed(held[half:], b_far[half:])


def merge_column_kernel(flags, b_right, b_left, b_opposite, grads, _, to_inner, to_outer, held, sems):
    rows = b_right.shape[0]
    (copy,) = fetch([(grads.at[pl.ds(2 * rows, 2 * rows)], held)], sems)
    shares = [ref[...].astype(jnp.float32) for ref in (b_right, b_left, b_opposite)]
    weights = [flags[k].astype(jnp.float32) for k in range(3)]
    part = shares[0] * weights[0] + shares[1] * weights[1] + shares[2] * weights[2]
    rest = (shares[0] + shares[1]) + (shares[2] - part)
    copy.wait()
    to_inner[...] = (held[:rows].astype(jnp.float32) + part).astype(jnp.bfloat16)
    to_outer[...] = (held[rows:].astype(jnp.float32) + rest).astype(jnp.bfloat16)


def merge_near_kernel(right, left, b_right, b_left, to_right, to_left):
    half = right.shape[0] // 2
    to_right[:half] = summed(right[:half], b_right[...])
    to_right[half:] = right[half:]
    to_left[:half] = left[:half]
    to_left[half:] = summed(left[half:], b_left[...])


def write_losses(losses, out, at):
    count, width = losses.shape[1], out.shape[1]
    high = losses.astype(jnp.bfloat16).astype(jnp.float32)
    row = lax.broadcasted_iota(jnp.int32, (16, count), 0)
    lines = jnp.where(row == 0, high, jnp.where(row == 1, losses - high, 0.0))
    out[at : at + 16, :count] = lines.astype(jnp.bfloat16)
    if width > count:
        out[at : at + 16, count:] = jnp.zeros((16, width - count), jnp.bfloat16)


def read_losses(ref, at, count):
    return jnp.sum(ref[at : at + 16, :count].astype(jnp.float32), axis=0, keepdims=True)


def image_kernel(counts, flags, scalars, before, near, b_up, b_down, *refs):
    k, n = len(counts), sum(counts)
    slopes, texts, refs = refs[:k], refs[k : k + n], refs[k + n :]
    sent, kept, g_right, g_left, *refs = refs
    before_held, slopes_held, texts_held, sides, sems = refs
    rows, count = texts_held.shape[0] // n, slopes_held.shape[1]
    groups, used, at, first = [], 0, 0, 0
    for s, m in zip(slopes, counts):
        moves = [(s, slopes_held.at[pl.ds(at, m * rows + 16)])]
        for j in range(first, first + m):
            block = texts[j].at[pl.ds(texts[j].shape[0] - rows, rows)]
            moves.append((block, texts_held.at[pl.ds(j * rows, rows)]))
        at += m * rows + 16
        first += m
        groups.append((moves, used))
        used += len(moves)
    rest = [(before, before_held), (near.at[pl.ds(0, 2 * rows)], sides)]
    groups.append((rest, used))
    groups = [
        [pltpu.make_async_copy(*pair, sems.at[base + i]) for i, pair in enumerate(moves)]
        for moves, base in groups
    ]
    for group in groups:
        for copy in group:
            copy.start()
    total, at, first, lines = None, 0, 0, []
    middle = k // 2
    for part in ((0, middle), (middle, k)):
        for group in groups[part[0] : part[1]]:
            for copy in group:
                copy.wait()
        every, start = [], first
        for m in counts[part[0] : part[1]]:
            every.append(slopes_held[at : at + m * rows, :])
            lines.append(at + m * rows)
            at += m * rows + 16
            first += m
        share = lax.dot_general(
            jnp.concatenate(every, axis=0), texts_held[start * rows : first * rows, :],
            (((0,), (0,)), ((), ())), preferred_element_type=jnp.float32,
        )
        total = share if total is None else total + share
    for copy in groups[-1]:
        copy.wait()
    g_right[...] = summed(sides[:rows, :], b_up[...])
    g_left[...] = summed(sides[rows:, :], b_down[...])
    before_held[:count, :] = (before_held[:count, :] + total) * scalars[2]
    loss = before_held[count:, :count]
    for line in lines:
        both = slopes_held[line : line + 16, :].astype(jnp.float32)
        loss = loss + (both[:8] + both[8:])
    loss = jnp.sum(loss, axis=0, keepdims=True)
    for j in range(2):
        here = slice(j * rows, (j + 1) * rows)
        mine, other = ((c + 2 * j) * rows for c in (flags[4], 1 - flags[4]))
        kept[here, :] = before_held[pl.ds(pl.multiple_of(mine, rows), rows), :]
        gone = before_held[pl.ds(pl.multiple_of(other, rows), rows), :]
        sent[here, :] = gone.astype(jnp.bfloat16)
    write_losses(loss, sent, 2 * rows)
    kept[2 * rows :, :count] = jnp.broadcast_to(loss, (8, count))


def image_gradient(flags, scalars, rows, before, slopes, texts, near, b_up, b_down):
    width = texts[0].shape[1]
    count = slopes[0].shape[1]
    counts = [(s.shape[0] - 16) // rows for s in slopes]
    return call(
        functools.partial(image_kernel, counts), "image_gradient",
        [shaped(2 * rows + 16, width), shaped(2 * rows + 8, width, dtype=jnp.float32)]
        + [shaped(rows, width)] * 2,
        flags, scalars, before, near, b_up, b_down, *slopes, *texts,
        limit=56,
        in_specs=[SMEM] * 2 + [ANY] * 2 + [VMEM] * 2 + [ANY] * (len(slopes) + len(texts)),
        scratch=[
            pltpu.VMEM((count + 8, width), jnp.float32),
            pltpu.VMEM((sum(s.shape[0] for s in slopes), count), jnp.bfloat16),
            pltpu.VMEM((len(texts) * rows, width), jnp.bfloat16),
            pltpu.VMEM((2 * rows, width), jnp.bfloat16),
            pltpu.SemaphoreType.DMA((2 + len(slopes) + len(texts),)),
        ],
    )


def half_kernel(flags, kept, received, _, mine, sent, loss_out):
    rows, count = mine.shape[0], loss_out.shape[1]

    def summed_core(h):
        here = pl.ds(pl.multiple_of(h * rows, rows), rows)
        return kept[here, :] + received[here, :].astype(jnp.float32)

    mine[...] = summed_core(flags[3])
    sent[:rows] = summed_core(1 - flags[3]).astype(jnp.bfloat16)
    both = kept[2 * rows : 2 * rows + 1, :count] + read_losses(received, 2 * rows, count)
    loss_out[...] = both
    write_losses(both, sent, rows)


def loss_kernel(loss, received, _, out):
    out[...] = loss[...] + read_losses(received, received.shape[0] - 16, loss.shape[1])


def last_kernel(n, values, kept, *refs):
    grads, (out, kept_held, held, sems) = refs[:n], refs[-4:]
    rows = values.shape[0]
    half = rows // 4
    (copy,) = fetch([(kept, kept_held)], sems)
    inverses = inverse_norms(values[...].astype(jnp.float32))
    copy.wait()
    copies = []
    for j in range(4):
        here = slice(j * half, (j + 1) * half)
        wide = values[here, :].astype(jnp.float32)
        inverse = inverses[here, :]
        unit = wide * inverse
        grad = total_of(kept_held[here, :], *[g[here, :] for g in grads])
        along = jnp.sum(unit * grad, axis=1, keepdims=True)
        held[here, :] = (grad - unit * along) * inverse
        window = pl.ds(j * half, half)
        copies.append(
            pltpu.make_async_copy(held.at[window], out.at[window], sems.at[1 + j])
        )
        copies[-1].start()
    for copy in copies:
        copy.wait()


def projected(values, kept, *grads, after=()):
    rows, width = values.shape
    return call(
        functools.partial(last_kernel, len(grads)), "project",
        [shaped(rows, width, dtype=jnp.float32)],
        values, kept, *grads, *after,
        in_specs=[VMEM, ANY] + [VMEM] * len(grads) + [ANY] * len(after),
        out_specs=[ANY],
        scratch=[
            pltpu.VMEM((rows, width), kept.dtype),
            pltpu.VMEM((rows, width), jnp.float32),
            pltpu.SemaphoreType.DMA((5,)),
        ],
    )[0]


def total_of(*parts):
    total = parts[0].astype(jnp.float32)
    for part in parts[1:]:
        total = total + part.astype(jnp.float32)
    return total


def summed(*parts):
    return total_of(*parts).astype(jnp.bfloat16)


def on_device(picture_vectors, caption_vectors, scale_exponent, offset_addend):
    rows, width = caption_vectors.shape
    count = picture_vectors.shape[0]
    half = rows // 2
    b, rep = lax.axis_index("blk"), lax.axis_index("rep")
    x, q, h, c = b % 4, (b // 4) % 2, rep // 2, rep % 2
    scale = jnp.exp(scale_exponent)
    scalars = jnp.concatenate([scale * LOG2E, offset_addend * LOG2E, scale])
    first = (rep * rows).astype(jnp.int32)[None]
    flags = [(x == 0) & (q == 0), (x == 3) & (q == 1), (x >= 2) & (q == 1), h, c]
    flags = jnp.stack([flag.astype(jnp.int32) for flag in flags])
    kernel = functools.partial(pairs, scalars, first, rows)

    own = normalised(caption_vectors)
    outer = move(own, OUTER)
    right, left = move(own, RIGHT), move(own, LEFT)
    inner = move(own, FLIP)
    images = normalised(picture_vectors)
    block, piece = shaped(rows, width), shaped(half, width)
    packet = shaped(rows + half, width)
    (g_own,), total = kernel(images, [own], own=True, sums=1)
    to_left, to_right = call(
        pack_kernel, "pack", [packet, packet], flags, outer, g_own, right, left, inner,
        in_specs=[SMEM, VMEM, ANY] + [VMEM] * 3,
    )
    from_right, from_left = move(to_left, RIGHT), move(to_right, LEFT)
    up, down = move(right, IN_UP), move(left, IN_DOWN)
    (g_near,), total = kernel(
        images, [right, left, inner, outer], joined=True, sums=2, before=(total,)
    )
    far, to_far = call(
        unpack_kernel, "unpack", [block] * 2,
        flags, g_near, from_right, from_left, inner, outer,
        in_specs=[SMEM, ANY] + [VMEM] * 4,
    )
    far_inner, far_outer = move(far, IN_FAR), move(to_far, OPPOSITE)
    (g_far, g_up, g_down, g_out_right, g_out_left), s_near = kernel(
        images, [far, up, down, from_right, from_left]
    )
    (g_far_inner, g_far_outer), s_far = kernel(
        images, [far_inner, far_outer], after=(s_near,)
    )

    def back(value, perm):
        return move(value, backwards(perm))

    b_up, b_down = back(g_up, IN_UP), back(g_down, IN_DOWN)
    b_out_right, b_out_left = back(g_out_right, RIGHT), back(g_out_left, LEFT)
    b_far_inner, b_far_outer = back(g_far_inner, IN_FAR), back(g_far_outer, OPPOSITE)
    held = [pltpu.VMEM((2 * rows, width), jnp.bfloat16), pltpu.SemaphoreType.DMA((1,))]
    sent, kept, g_right, g_left = image_gradient(
        flags, scalars, rows, total,
        [s_near, s_far],
        [far, up, down, from_right, from_left, far_inner, far_outer],
        g_near, b_up, b_down,
    )
    received = move(sent, CORE)
    wide = shaped(rows, width, dtype=jnp.float32)
    to_right, to_left = call(
        merge_far_kernel, "merge_far", [piece] * 2,
        b_far_inner, g_far, b_far_outer, b_out_right, b_out_left,
        in_specs=[VMEM] + [ANY] * 4,
        scratch=[pltpu.VMEM((rows, width), jnp.bfloat16), pltpu.SemaphoreType.DMA((1,))],
        flops=20_000_000_000,
    )
    g_inner, g_outer = call(
        merge_column_kernel, "merge_column", [block] * 2,
        flags, b_out_right, b_out_left, b_far_outer, g_near, to_left,
        in_specs=[SMEM] + [VMEM] * 3 + [ANY] * 2, scratch=held,
    )
    b_right, b_left = back(to_right, RIGHT), back(to_left, LEFT)
    mine, sent, loss = call(
        half_kernel, "half", [wide, shaped(rows + 16, width), shaped(1, count, dtype=jnp.float32)],
        flags, kept, received, to_left,
        in_specs=[SMEM, VMEM, VMEM, ANY],
    )
    received = move(sent, HALF)
    g_right, g_left = call(
        merge_near_kernel, "merge_near", [block] * 2, g_right, g_left, b_right, b_left
    )
    b_right, b_left = back(g_right, RIGHT), back(g_left, LEFT)
    b_inner, b_outer = back(g_inner, FLIP), back(g_outer, OUTER)
    pictures = lax.dynamic_slice_in_dim(picture_vectors, rep * rows, rows, 0)
    grad_images = projected(pictures, mine, received[:rows])
    (loss,) = call(
        loss_kernel, "losses", [loss], loss, received, grad_images, in_specs=[VMEM, VMEM, ANY]
    )
    loss_rows = lax.dynamic_slice_in_dim(loss[0], rep * rows, rows, 0) / (12 * count)
    grad_texts = projected(
        caption_vectors, g_own, b_right, b_left, b_inner, b_outer, after=(loss,)
    )
    return grad_images, grad_texts, loss_rows


def solution(mesh):
    in_specs = (P("blk", None), P(("blk", "rep"), None), P(), P())
    out_specs = (P(("blk", "rep"), None), P(("blk", "rep"), None), P(("blk", "rep")))
    return jax.shard_map(
        on_device, mesh=mesh, in_specs=in_specs, out_specs=out_specs, check_vma=False
    )
```

```python
import functools
import math

import jax
import jax.numpy as jnp
from jax import lax
from jax.experimental import pallas as pl
from jax.experimental.pallas import tpu as pltpu
from jax.sharding import PartitionSpec as P

EPS = 1e-06
LOG2E = math.log2(math.e)
LN2 = math.log(2.0)
AXES = ("blk", "rep")
NZ, NX = 8, 4
VMEM = pl.BlockSpec(memory_space=pltpu.VMEM)
SMEM = pl.BlockSpec(memory_space=pltpu.SMEM)
ANY = pl.BlockSpec(memory_space=pl.ANY)


def decode(i):
    b, r = divmod(i, 4)
    z, p = divmod(b, 8)
    q, x = divmod(p, 4)
    h, c = divmod(r, 2)
    return z, q, x, h, c


def encode(z, q, x, h, c):
    return ((z % NZ) * 8 + q * 4 + (x % NX)) * 4 + h * 2 + c


def received_from(source):
    return [(encode(*source(*decode(i))), i) for i in range(NZ * 8 * 4)]


def backwards(perm):
    return [(d, s) for s, d in perm]


def flip(z, q, x, h, c):
    return z, 1 - q, x, h ^ c, c


def outer(z, q, x, h, c):
    return (z - 1 if q == 0 else z + 1), 1 - q, x, h ^ c, c


def x_shift(d):
    return received_from(lambda z, q, x, h, c: (z, q, x + d, h, c))


def in_plane_up(z, q, x, h, c):
    return (z + 1, q, x, h, c) if x == 3 else flip(z, q, x, h, c)


def in_plane_down(z, q, x, h, c):
    return (z - 1, q, x, h, c) if x == 0 else flip(z, q, x, h, c)


def in_plane_far(z, q, x, h, c):
    return (z - 1, q, x, h, c) if x <= 1 else flip(z, q, x, h, c)


LEFT, RIGHT = x_shift(-1), x_shift(1)
FLIP, OUTER = received_from(flip), received_from(outer)
IN_UP, IN_DOWN, IN_FAR = (received_from(f) for f in (in_plane_up, in_plane_down, in_plane_far))
OPPOSITE = x_shift(2)
CORE = received_from(lambda z, q, x, h, c: (z, q, x, h, 1 - c))
HALF = received_from(lambda z, q, x, h, c: (z, q, x, 1 - h, c))


def move(value, perm):
    return lax.ppermute(value, AXES, perm)


def call(
    kernel, name, outs, *args,
    scalars=0, limit=16, in_specs=None, out_specs=None, scratch=(), flops=1,
):
    return pl.pallas_call(
        kernel,
        out_shape=[jax.ShapeDtypeStruct(out.shape, out.dtype) for out in outs],
        in_specs=in_specs or [SMEM] * scalars + [VMEM] * (len(args) - scalars),
        out_specs=out_specs or [VMEM] * len(outs),
        scratch_shapes=list(scratch),
        compiler_params=pltpu.CompilerParams(vmem_limit_bytes=limit << 20),
        cost_estimate=pl.CostEstimate(flops=flops, bytes_accessed=1, transcendentals=0),
        name=name,
    )(*args)


def shaped(*shape, dtype=jnp.bfloat16):
    return jax.ShapeDtypeStruct(shape, dtype)


def inverse_norms(wide):
    return 1.0 / jnp.sqrt(jnp.sum(wide * wide, axis=1, keepdims=True) + EPS)


def normalise_kernel(values, out):
    rows = values.shape[0]
    step = min(rows, 192)
    for at in range(0, rows, step):
        wide = values[at : at + step, :].astype(jnp.float32)
        out[at : at + step, :] = (wide * inverse_norms(wide)).astype(jnp.bfloat16)


def normalised(values):
    return call(normalise_kernel, "normalise", [shaped(*values.shape)], values)[0]


def last_rows(ref, rows):
    return ref[ref.shape[0] - rows :, :]


def pairs_kernel(n, rows, own, joined, sums, scalars, first, images, *refs):
    if own:
        (flags, *refs), flags_out = refs[:-1], refs[-1]
        for k in range(5):
            flags_out[k] = flags[k]
    texts, last = refs[:n], refs[-1]
    grads = refs[-2:-1] if joined else refs[-n - 1 : -1]
    factor, addend, scale = scalars[0], scalars[1], scalars[2]
    image = images[...]
    count = image.shape[0]
    block = jnp.concatenate([last_rows(text, rows) for text in texts], axis=0)
    cosines = lax.dot_general(
        block, image, (((1,), (1,)), ((), ())), preferred_element_type=jnp.float32
    )
    t = cosines * factor + addend
    if own:
        text_row = lax.broadcasted_iota(jnp.int32, t.shape, 0) + first[0]
        matched = text_row == lax.broadcasted_iota(jnp.int32, t.shape, 1)
        t = jnp.where(matched, -t, t)
    e = jnp.exp2(t)
    u = 1.0 + e
    r = pl.reciprocal(u, approx=True)
    slopes = e * r
    lost = (e - (u - 1.0)) * r
    q = n * rows // 4
    product = (u[:q] * u[q : 2 * q]) * (u[2 * q : 3 * q] * u[3 * q :])
    lost = (lost[:q] + lost[q : 2 * q]) + (lost[2 * q : 3 * q] + lost[3 * q :])
    losses = jnp.log2(product) * LN2 + lost
    total = jnp.sum(losses.reshape(q // 8, 8, count), axis=0)
    if own:
        slopes = jnp.where(matched, -slopes, slopes)
    slopes = slopes.astype(jnp.bfloat16)
    grad = jnp.dot(slopes, image, preferred_element_type=jnp.float32)
    grad = (grad * scale).astype(jnp.bfloat16)
    if joined:
        grads[0][...] = grad
    else:
        for k in range(n):
            grads[k][...] = grad[k * rows : (k + 1) * rows]
    if sums == 0:
        last[: n * rows, :] = slopes
        high = total.astype(jnp.bfloat16)
        low = (total - high.astype(jnp.float32)).astype(jnp.bfloat16)
        last[n * rows :, :] = jnp.concatenate([high, low], axis=0)
        return
    share = lax.dot_general(
        slopes, block, (((0,), (0,)), ((), ())), preferred_element_type=jnp.float32
    )
    before = refs[n] if sums == 2 else None
    last[:count, :] = before[:count, :] + share if sums == 2 else share
    last[count:, :count] = before[count:, :count] + total if sums == 2 else total


def pairs(
    scalars, first, rows, images, texts, after=(), own=(), joined=False, sums=0, before=()
):
    n, width = len(texts), images.shape[1]
    count = images.shape[0]
    outs = [shaped(n * rows, width)] if joined else [shaped(rows, width)] * n
    if sums:
        outs.append(shaped(count + 8, width, dtype=jnp.float32))
    else:
        outs.append(shaped(n * rows + 16, count))
    outs += [shaped(5, dtype=jnp.int32)] * len(own)
    out = call(
        functools.partial(pairs_kernel, n, rows, bool(own), joined, sums), f"pairs_{n}", outs,
        scalars, first, images, *own, *texts, *before, *after,
        in_specs=[SMEM] * 2 + [VMEM] + [SMEM] * len(own) + [VMEM] * (n + len(before))
        + [ANY] * len(after),
        out_specs=[VMEM] * (len(outs) - len(own)) + [SMEM] * len(own),
    )
    if own:
        return out[:-2], out[-2], out[-1]
    return out[:-1], out[-1]


def choose(flag, first, second, out, at):
    @pl.when(flag == 1)
    def _():
        out[at:] = first[...]

    @pl.when(flag == 0)
    def _():
        out[at:] = second[...]


def pack_kernel(flags, right, left, inner, outer, to_left, to_right):
    half = right.shape[0] // 2
    to_left[:half] = right[:half]
    to_right[:half] = left[half:]
    choose(flags[0], inner, outer, to_left, half)
    choose(flags[1], inner, outer, to_right, half)


def unpack_kernel(flags, _, from_right, from_left, inner, outer, far, to_far):
    half = far.shape[0] // 2
    far[:half] = from_right[:half]
    far[half:] = from_left[:half]
    choose(flags[2], inner, outer, to_far, 0)


def fetch(pairs_of_refs, sems):
    copies = [pltpu.make_async_copy(*pair, sems.at[k]) for k, pair in enumerate(pairs_of_refs)]
    for copy in copies:
        copy.start()
    return copies


def merge_far_kernel(b_far, far, *refs):
    to_right, to_left, held, sems = refs[-4:]
    half = b_far.shape[0] // 2
    (copy,) = fetch([(far, held)], sems)
    copy.wait()
    to_right[...] = summed(held[:half], b_far[:half])
    to_left[...] = summed(held[half:], b_far[half:])


def merge_column_kernel(flags, b_right, b_left, b_opposite, grads, _, to_inner, to_outer, held, sems):
    rows = b_right.shape[0]
    (copy,) = fetch([(grads.at[pl.ds(2 * rows, 2 * rows)], held)], sems)
    shares = [ref[...].astype(jnp.float32) for ref in (b_right, b_left, b_opposite)]
    weights = [flags[k].astype(jnp.float32) for k in range(3)]
    part = shares[0] * weights[0] + shares[1] * weights[1] + shares[2] * weights[2]
    rest = (shares[0] + shares[1]) + (shares[2] - part)
    copy.wait()
    to_inner[...] = (held[:rows].astype(jnp.float32) + part).astype(jnp.bfloat16)
    to_outer[...] = (held[rows:].astype(jnp.float32) + rest).astype(jnp.bfloat16)


def merge_near_kernel(right, left, b_right, b_left, to_right, to_left):
    half = right.shape[0] // 2
    to_right[:half] = summed(right[:half], b_right[...])
    to_right[half:] = right[half:]
    to_left[:half] = left[:half]
    to_left[half:] = summed(left[half:], b_left[...])


def write_losses(losses, out, at):
    count, width = losses.shape[1], out.shape[1]
    high = losses.astype(jnp.bfloat16).astype(jnp.float32)
    row = lax.broadcasted_iota(jnp.int32, (16, count), 0)
    lines = jnp.where(row == 0, high, jnp.where(row == 1, losses - high, 0.0))
    out[at : at + 16, :count] = lines.astype(jnp.bfloat16)
    if width > count:
        out[at : at + 16, count:] = jnp.zeros((16, width - count), jnp.bfloat16)


def read_losses(ref, at, count):
    return jnp.sum(ref[at : at + 16, :count].astype(jnp.float32), axis=0, keepdims=True)


def image_kernel(counts, flags, scalars, before, near, b_up, b_down, *refs):
    k, n = len(counts), sum(counts)
    slopes, texts, refs = refs[:k], refs[k : k + n], refs[k + n :]
    sent, kept, g_right, g_left, *refs = refs
    before_held, slopes_held, texts_held, sides, sems = refs
    rows, count = texts_held.shape[0] // n, slopes_held.shape[1]
    groups, used, at, first = [], 0, 0, 0
    for s, m in zip(slopes, counts):
        moves = [(s, slopes_held.at[pl.ds(at, m * rows + 16)])]
        for j in range(first, first + m):
            block = texts[j].at[pl.ds(texts[j].shape[0] - rows, rows)]
            moves.append((block, texts_held.at[pl.ds(j * rows, rows)]))
        at += m * rows + 16
        first += m
        groups.append((moves, used))
        used += len(moves)
    rest = [(before, before_held), (near.at[pl.ds(0, 2 * rows)], sides)]
    groups.append((rest, used))
    groups = [
        [pltpu.make_async_copy(*pair, sems.at[base + i]) for i, pair in enumerate(moves)]
        for moves, base in groups
    ]
    for group in groups:
        for copy in group:
            copy.start()
    spans, lines, at, first = [], [], 0, 0
    for m in counts:
        spans.append((slice(at, at + m * rows), slice(first * rows, (first + m) * rows)))
        lines.append(slice(at + m * rows, at + m * rows + 16))
        at += m * rows + 16
        first += m
    for h in range(2):
        total = None
        columns = slice(2 * h * rows, 2 * (h + 1) * rows)
        for group, (slope_rows, text_rows) in zip(groups, spans):
            if h == 0:
                for copy in group:
                    copy.wait()
            share = lax.dot_general(
                slopes_held[slope_rows, columns], texts_held[text_rows, :],
                (((0,), (0,)), ((), ())), preferred_element_type=jnp.float32,
            )
            total = share if total is None else total + share
        if h == 0:
            for copy in groups[-1]:
                copy.wait()
        before_held[columns, :] = (before_held[columns, :] + total) * scalars[2]
        mine, other = ((c + 2 * h) * rows for c in (flags[4], 1 - flags[4]))
        here = slice(h * rows, (h + 1) * rows)
        kept[here, :] = before_held[pl.ds(pl.multiple_of(mine, rows), rows), :]
        gone = before_held[pl.ds(pl.multiple_of(other, rows), rows), :]
        sent[here, :] = gone.astype(jnp.bfloat16)
    g_right[...] = summed(sides[:rows, :], b_up[...])
    g_left[...] = summed(sides[rows:, :], b_down[...])
    loss = before_held[count:, :count]
    for line in lines:
        both = slopes_held[line, :].astype(jnp.float32)
        loss = loss + (both[:8] + both[8:])
    loss = jnp.sum(loss, axis=0, keepdims=True)
    write_losses(loss, sent, 2 * rows)
    kept[2 * rows :, :count] = jnp.broadcast_to(loss, (8, count))


def image_gradient(flags, scalars, rows, before, slopes, texts, near, b_up, b_down):
    width = texts[0].shape[1]
    count = slopes[0].shape[1]
    counts = [(s.shape[0] - 16) // rows for s in slopes]
    return call(
        functools.partial(image_kernel, counts), "image_gradient",
        [shaped(2 * rows + 16, width), shaped(2 * rows + 8, width, dtype=jnp.float32)]
        + [shaped(rows, width)] * 2,
        flags, scalars, before, near, b_up, b_down, *slopes, *texts,
        limit=56,
        in_specs=[SMEM] * 2 + [ANY] * 2 + [VMEM] * 2 + [ANY] * (len(slopes) + len(texts)),
        scratch=[
            pltpu.VMEM((count + 8, width), jnp.float32),
            pltpu.VMEM((sum(s.shape[0] for s in slopes), count), jnp.bfloat16),
            pltpu.VMEM((len(texts) * rows, width), jnp.bfloat16),
            pltpu.VMEM((2 * rows, width), jnp.bfloat16),
            pltpu.SemaphoreType.DMA((2 + len(slopes) + len(texts),)),
        ],
    )


def half_kernel(flags, kept, received, _, mine, sent, loss_out):
    rows, count = mine.shape[0], loss_out.shape[1]

    def summed_core(h):
        here = pl.ds(pl.multiple_of(h * rows, rows), rows)
        return kept[here, :] + received[here, :].astype(jnp.float32)

    mine[...] = summed_core(flags[3])
    sent[:rows] = summed_core(1 - flags[3]).astype(jnp.bfloat16)
    both = kept[2 * rows : 2 * rows + 1, :count] + read_losses(received, 2 * rows, count)
    loss_out[...] = both
    write_losses(both, sent, rows)


def loss_kernel(loss, received, _, out):
    out[...] = loss[...] + read_losses(received, received.shape[0] - 16, loss.shape[1])


def last_kernel(n, values, kept, *refs):
    grads, (out, kept_held, held, sems) = refs[:n], refs[-4:]
    rows = values.shape[0]
    half = rows // 4
    (copy,) = fetch([(kept, kept_held)], sems)
    inverses = inverse_norms(values[...].astype(jnp.float32))
    copy.wait()
    copies = []
    for j in range(4):
        here = slice(j * half, (j + 1) * half)
        wide = values[here, :].astype(jnp.float32)
        inverse = inverses[here, :]
        unit = wide * inverse
        grad = total_of(kept_held[here, :], *[g[here, :] for g in grads])
        along = jnp.sum(unit * grad, axis=1, keepdims=True)
        held[here, :] = (grad - unit * along) * inverse
        window = pl.ds(j * half, half)
        copies.append(
            pltpu.make_async_copy(held.at[window], out.at[window], sems.at[1 + j])
        )
        copies[-1].start()
    for copy in copies:
        copy.wait()


def projected(values, kept, *grads, after=()):
    rows, width = values.shape
    return call(
        functools.partial(last_kernel, len(grads)), "project",
        [shaped(rows, width, dtype=jnp.float32)],
        values, kept, *grads, *after,
        in_specs=[VMEM, ANY] + [VMEM] * len(grads) + [ANY] * len(after),
        out_specs=[ANY],
        scratch=[
            pltpu.VMEM((rows, width), kept.dtype),
            pltpu.VMEM((rows, width), jnp.float32),
            pltpu.SemaphoreType.DMA((5,)),
        ],
    )[0]


def total_of(*parts):
    total = parts[0].astype(jnp.float32)
    for part in parts[1:]:
        total = total + part.astype(jnp.float32)
    return total


def summed(*parts):
    return total_of(*parts).astype(jnp.bfloat16)


def on_device(picture_vectors, caption_vectors, scale_exponent, offset_addend):
    rows, width = caption_vectors.shape
    count = picture_vectors.shape[0]
    half = rows // 2
    b, rep = lax.axis_index("blk"), lax.axis_index("rep")
    x, q, h, c = b % 4, (b // 4) % 2, rep // 2, rep % 2
    scale = jnp.exp(scale_exponent)
    scalars = jnp.concatenate([scale * LOG2E, offset_addend * LOG2E, scale])
    first = (rep * rows).astype(jnp.int32)[None]
    flags = [(x == 0) & (q == 0), (x == 3) & (q == 1), (x >= 2) & (q == 1), h, c]
    flags = jnp.stack([flag.astype(jnp.int32) for flag in flags])
    kernel = functools.partial(pairs, scalars, first, rows)

    own = normalised(caption_vectors)
    outer = move(own, OUTER)
    right, left = move(own, RIGHT), move(own, LEFT)
    inner = move(own, FLIP)
    images = normalised(picture_vectors)
    block, piece = shaped(rows, width), shaped(half, width)
    packet = shaped(rows + half, width)
    (g_own,), total, flags = kernel(images, [own], own=(flags,), sums=1)
    to_left, to_right = call(
        pack_kernel, "pack", [packet, packet], flags, right, left, inner, outer, scalars=1,
    )
    from_right, from_left = move(to_left, RIGHT), move(to_right, LEFT)
    up, down = move(right, IN_UP), move(left, IN_DOWN)
    (g_near,), total = kernel(
        images, [right, left, inner, outer], joined=True, sums=2, before=(total,)
    )
    far, to_far = call(
        unpack_kernel, "unpack", [block] * 2,
        flags, g_near, from_right, from_left, inner, outer,
        in_specs=[SMEM, ANY] + [VMEM] * 4,
    )
    far_inner, far_outer = move(far, IN_FAR), move(to_far, OPPOSITE)
    (g_far, g_up, g_down, g_out_right, g_out_left), s_near = kernel(
        images, [far, up, down, from_right, from_left]
    )
    (g_far_inner, g_far_outer), s_far = kernel(
        images, [far_inner, far_outer], after=(s_near,)
    )

    def back(value, perm):
        return move(value, backwards(perm))

    b_up, b_down = back(g_up, IN_UP), back(g_down, IN_DOWN)
    b_out_right, b_out_left = back(g_out_right, RIGHT), back(g_out_left, LEFT)
    b_far_inner, b_far_outer = back(g_far_inner, IN_FAR), back(g_far_outer, OPPOSITE)
    held = [pltpu.VMEM((2 * rows, width), jnp.bfloat16), pltpu.SemaphoreType.DMA((1,))]
    sent, kept, g_right, g_left = image_gradient(
        flags, scalars, rows, total,
        [s_near, s_far],
        [far, up, down, from_right, from_left, far_inner, far_outer],
        g_near, b_up, b_down,
    )
    received = move(sent, CORE)
    wide = shaped(rows, width, dtype=jnp.float32)
    to_right, to_left = call(
        merge_far_kernel, "merge_far", [piece] * 2,
        b_far_inner, g_far, b_far_outer, b_out_right, b_out_left,
        in_specs=[VMEM] + [ANY] * 4,
        scratch=[pltpu.VMEM((rows, width), jnp.bfloat16), pltpu.SemaphoreType.DMA((1,))],
        flops=20_000_000_000,
    )
    g_inner, g_outer = call(
        merge_column_kernel, "merge_column", [block] * 2,
        flags, b_out_right, b_out_left, b_far_outer, g_near, to_left,
        in_specs=[SMEM] + [VMEM] * 3 + [ANY] * 2, scratch=held,
    )
    b_right, b_left = back(to_right, RIGHT), back(to_left, LEFT)
    mine, sent, loss = call(
        half_kernel, "half", [wide, shaped(rows + 16, width), shaped(1, count, dtype=jnp.float32)],
        flags, kept, received, to_left,
        in_specs=[SMEM, VMEM, VMEM, ANY],
    )
    received = move(sent, HALF)
    g_right, g_left = call(
        merge_near_kernel, "merge_near", [block] * 2, g_right, g_left, b_right, b_left
    )
    b_right, b_left = back(g_right, RIGHT), back(g_left, LEFT)
    b_inner, b_outer = back(g_inner, FLIP), back(g_outer, OUTER)
    pictures = lax.dynamic_slice_in_dim(picture_vectors, rep * rows, rows, 0)
    grad_images = projected(pictures, mine, received[:rows])
    (loss,) = call(
        loss_kernel, "losses", [loss], loss, received, grad_images, in_specs=[VMEM, VMEM, ANY]
    )
    loss_rows = lax.dynamic_slice_in_dim(loss[0], rep * rows, rows, 0) / (12 * count)
    grad_texts = projected(
        caption_vectors, g_own, b_right, b_left, b_inner, b_outer, after=(loss,)
    )
    return grad_images, grad_texts, loss_rows


def solution(mesh):
    in_specs = (P("blk", None), P(("blk", "rep"), None), P(), P())
    out_specs = (P(("blk", "rep"), None), P(("blk", "rep"), None), P(("blk", "rep")))
    return jax.shard_map(
        on_device, mesh=mesh, in_specs=in_specs, out_specs=out_specs, check_vma=False
    )
```

```python
import functools
import math

import jax
import jax.numpy as jnp
from jax import lax
from jax.experimental import pallas as pl
from jax.experimental.pallas import tpu as pltpu
from jax.sharding import PartitionSpec as P

EPS = 1e-06
LOG2E = math.log2(math.e)
LN2 = math.log(2.0)
AXES = ("blk", "rep")
NZ, NX = 8, 4
VMEM = pl.BlockSpec(memory_space=pltpu.VMEM)
SMEM = pl.BlockSpec(memory_space=pltpu.SMEM)
ANY = pl.BlockSpec(memory_space=pl.ANY)


def decode(i):
    b, r = divmod(i, 4)
    z, p = divmod(b, 8)
    q, x = divmod(p, 4)
    h, c = divmod(r, 2)
    return z, q, x, h, c


def encode(z, q, x, h, c):
    return ((z % NZ) * 8 + q * 4 + (x % NX)) * 4 + h * 2 + c


def received_from(source):
    return [(encode(*source(*decode(i))), i) for i in range(NZ * 8 * 4)]


def backwards(perm):
    return [(d, s) for s, d in perm]


def flip(z, q, x, h, c):
    return z, 1 - q, x, h ^ c, c


def outer(z, q, x, h, c):
    return (z - 1 if q == 0 else z + 1), 1 - q, x, h ^ c, c


def x_shift(d):
    return received_from(lambda z, q, x, h, c: (z, q, x + d, h, c))


def in_plane_up(z, q, x, h, c):
    return (z + 1, q, x, h, c) if x == 3 else flip(z, q, x, h, c)


def in_plane_down(z, q, x, h, c):
    return (z - 1, q, x, h, c) if x == 0 else flip(z, q, x, h, c)


def in_plane_far(z, q, x, h, c):
    return (z - 1, q, x, h, c) if x <= 1 else flip(z, q, x, h, c)


LEFT, RIGHT = x_shift(-1), x_shift(1)
FLIP, OUTER = received_from(flip), received_from(outer)
IN_UP, IN_DOWN, IN_FAR = (received_from(f) for f in (in_plane_up, in_plane_down, in_plane_far))
OPPOSITE = x_shift(2)
CORE = received_from(lambda z, q, x, h, c: (z, q, x, h, 1 - c))
HALF = received_from(lambda z, q, x, h, c: (z, q, x, 1 - h, c))


def move(value, perm):
    return lax.ppermute(value, AXES, perm)


def call(
    kernel, name, outs, *args,
    scalars=0, limit=16, in_specs=None, out_specs=None, scratch=(), flops=1,
):
    return pl.pallas_call(
        kernel,
        out_shape=[jax.ShapeDtypeStruct(out.shape, out.dtype) for out in outs],
        in_specs=in_specs or [SMEM] * scalars + [VMEM] * (len(args) - scalars),
        out_specs=out_specs or [VMEM] * len(outs),
        scratch_shapes=list(scratch),
        compiler_params=pltpu.CompilerParams(vmem_limit_bytes=limit << 20),
        cost_estimate=pl.CostEstimate(flops=flops, bytes_accessed=1, transcendentals=0),
        name=name,
    )(*args)


def shaped(*shape, dtype=jnp.bfloat16):
    return jax.ShapeDtypeStruct(shape, dtype)


def inverse_norms(wide):
    return 1.0 / jnp.sqrt(jnp.sum(wide * wide, axis=1, keepdims=True) + EPS)


def normalise_kernel(values, out):
    rows = values.shape[0]
    step = min(rows, 192)
    for at in range(0, rows, step):
        wide = values[at : at + step, :].astype(jnp.float32)
        out[at : at + step, :] = (wide * inverse_norms(wide)).astype(jnp.bfloat16)


def fetch_and_normalise_kernel(values, out, held, sems):
    (copy,) = fetch([(values, held)], sems)
    copy.wait()
    normalise_kernel(held, out)


def fetched_and_normalised(values):
    return call(
        fetch_and_normalise_kernel, "normalise_own", [shaped(*values.shape)], values,
        limit=60, in_specs=[ANY],
        scratch=[pltpu.VMEM(values.shape, values.dtype), pltpu.SemaphoreType.DMA((1,))],
    )[0]


def normalised(values):
    return call(normalise_kernel, "normalise", [shaped(*values.shape)], values)[0]


def last_rows(ref, rows):
    return ref[ref.shape[0] - rows :, :]


def pairs_kernel(n, rows, own, joined, sums, scalars, first, images, *refs):
    if own:
        (flags, *refs), flags_out = refs[:-1], refs[-1]
        for k in range(5):
            flags_out[k] = flags[k]
    texts, last = refs[:n], refs[-1]
    grads = refs[-2:-1] if joined else refs[-n - 1 : -1]
    factor, addend, scale = scalars[0], scalars[1], scalars[2]
    image = images[...]
    count = image.shape[0]
    block = jnp.concatenate([last_rows(text, rows) for text in texts], axis=0)
    cosines = lax.dot_general(
        block, image, (((1,), (1,)), ((), ())), preferred_element_type=jnp.float32
    )
    t = cosines * factor + addend
    if own:
        text_row = lax.broadcasted_iota(jnp.int32, t.shape, 0) + first[0]
        matched = text_row == lax.broadcasted_iota(jnp.int32, t.shape, 1)
        t = jnp.where(matched, -t, t)
    e = jnp.exp2(t)
    u = 1.0 + e
    r = pl.reciprocal(u, approx=True)
    slopes = e * r
    lost = (e - (u - 1.0)) * r
    q = n * rows // 4
    product = (u[:q] * u[q : 2 * q]) * (u[2 * q : 3 * q] * u[3 * q :])
    lost = (lost[:q] + lost[q : 2 * q]) + (lost[2 * q : 3 * q] + lost[3 * q :])
    losses = jnp.log2(product) * LN2 + lost
    total = jnp.sum(losses.reshape(q // 8, 8, count), axis=0)
    if own:
        slopes = jnp.where(matched, -slopes, slopes)
    slopes = slopes.astype(jnp.bfloat16)
    grad = jnp.dot(slopes, image, preferred_element_type=jnp.float32)
    grad = (grad * scale).astype(jnp.bfloat16)
    if joined:
        grads[0][...] = grad
    else:
        for k in range(n):
            grads[k][...] = grad[k * rows : (k + 1) * rows]
    if sums == 0:
        last[: n * rows, :] = slopes
        high = total.astype(jnp.bfloat16)
        low = (total - high.astype(jnp.float32)).astype(jnp.bfloat16)
        last[n * rows :, :] = jnp.concatenate([high, low], axis=0)
        return
    share = lax.dot_general(
        slopes, block, (((0,), (0,)), ((), ())), preferred_element_type=jnp.float32
    )
    before = refs[n] if sums == 2 else None
    last[:count, :] = before[:count, :] + share if sums == 2 else share
    last[count:, :count] = before[count:, :count] + total if sums == 2 else total


def pairs(
    scalars, first, rows, images, texts, after=(), own=(), joined=False, sums=0, before=()
):
    n, width = len(texts), images.shape[1]
    count = images.shape[0]
    outs = [shaped(n * rows, width)] if joined else [shaped(rows, width)] * n
    if sums:
        outs.append(shaped(count + 8, width, dtype=jnp.float32))
    else:
        outs.append(shaped(n * rows + 16, count))
    outs += [shaped(5, dtype=jnp.int32)] * len(own)
    out = call(
        functools.partial(pairs_kernel, n, rows, bool(own), joined, sums), f"pairs_{n}", outs,
        scalars, first, images, *own, *texts, *before, *after,
        in_specs=[SMEM] * 2 + [VMEM] + [SMEM] * len(own) + [VMEM] * (n + len(before))
        + [ANY] * len(after),
        out_specs=[VMEM] * (len(outs) - len(own)) + [SMEM] * len(own),
    )
    if own:
        return out[:-2], out[-2], out[-1]
    return out[:-1], out[-1]


def choose(flag, first, second, out, at):
    @pl.when(flag == 1)
    def _():
        out[at:] = first[...]

    @pl.when(flag == 0)
    def _():
        out[at:] = second[...]


def pack_kernel(flags, right, left, inner, outer, to_left, to_right):
    half = right.shape[0] // 2
    to_left[:half] = right[:half]
    to_right[:half] = left[half:]
    choose(flags[0], inner, outer, to_left, half)
    choose(flags[1], inner, outer, to_right, half)


def unpack_kernel(flags, _, from_right, from_left, inner, outer, far, to_far):
    half = far.shape[0] // 2
    far[:half] = from_right[:half]
    far[half:] = from_left[:half]
    choose(flags[2], inner, outer, to_far, 0)


def fetch(pairs_of_refs, sems):
    copies = [pltpu.make_async_copy(*pair, sems.at[k]) for k, pair in enumerate(pairs_of_refs)]
    for copy in copies:
        copy.start()
    return copies


def merge_far_kernel(b_far, far, *refs):
    to_right, to_left, held, sems = refs[-4:]
    half = b_far.shape[0] // 2
    (copy,) = fetch([(far, held)], sems)
    copy.wait()
    to_right[...] = summed(held[:half], b_far[:half])
    to_left[...] = summed(held[half:], b_far[half:])


def merge_column_kernel(flags, b_right, b_left, b_opposite, grads, _, to_inner, to_outer, held, sems):
    rows = b_right.shape[0]
    (copy,) = fetch([(grads.at[pl.ds(2 * rows, 2 * rows)], held)], sems)
    shares = [ref[...].astype(jnp.float32) for ref in (b_right, b_left, b_opposite)]
    weights = [flags[k].astype(jnp.float32) for k in range(3)]
    part = shares[0] * weights[0] + shares[1] * weights[1] + shares[2] * weights[2]
    rest = (shares[0] + shares[1]) + (shares[2] - part)
    copy.wait()
    to_inner[...] = (held[:rows].astype(jnp.float32) + part).astype(jnp.bfloat16)
    to_outer[...] = (held[rows:].astype(jnp.float32) + rest).astype(jnp.bfloat16)


def merge_near_kernel(right, left, b_right, b_left, to_right, to_left):
    half = right.shape[0] // 2
    to_right[:half] = summed(right[:half], b_right[...])
    to_right[half:] = right[half:]
    to_left[:half] = left[:half]
    to_left[half:] = summed(left[half:], b_left[...])


def write_losses(losses, out, at):
    count, width = losses.shape[1], out.shape[1]
    high = losses.astype(jnp.bfloat16).astype(jnp.float32)
    row = lax.broadcasted_iota(jnp.int32, (16, count), 0)
    lines = jnp.where(row == 0, high, jnp.where(row == 1, losses - high, 0.0))
    out[at : at + 16, :count] = lines.astype(jnp.bfloat16)
    if width > count:
        out[at : at + 16, count:] = jnp.zeros((16, width - count), jnp.bfloat16)


def read_losses(ref, at, count):
    return jnp.sum(ref[at : at + 16, :count].astype(jnp.float32), axis=0, keepdims=True)


def image_kernel(counts, flags, scalars, before, near, b_up, b_down, *refs):
    k, n = len(counts), sum(counts)
    slopes, texts, refs = refs[:k], refs[k : k + n], refs[k + n :]
    sent, kept, g_right, g_left, *refs = refs
    before_held, slopes_held, texts_held, sides, sems = refs
    rows, count = texts_held.shape[0] // n, slopes_held.shape[1]
    groups, used, at, first = [], 0, 0, 0
    for s, m in zip(slopes, counts):
        moves = [(s, slopes_held.at[pl.ds(at, m * rows + 16)])]
        for j in range(first, first + m):
            block = texts[j].at[pl.ds(texts[j].shape[0] - rows, rows)]
            moves.append((block, texts_held.at[pl.ds(j * rows, rows)]))
        at += m * rows + 16
        first += m
        groups.append((moves, used))
        used += len(moves)
    rest = [(before, before_held), (near.at[pl.ds(0, 2 * rows)], sides)]
    groups.append((rest, used))
    groups = [
        [pltpu.make_async_copy(*pair, sems.at[base + i]) for i, pair in enumerate(moves)]
        for moves, base in groups
    ]
    for group in groups:
        for copy in group:
            copy.start()
    spans, lines, at, first = [], [], 0, 0
    for m in counts:
        spans.append((slice(at, at + m * rows), slice(first * rows, (first + m) * rows)))
        lines.append(slice(at + m * rows, at + m * rows + 16))
        at += m * rows + 16
        first += m
    for h in range(2):
        total = None
        columns = slice(2 * h * rows, 2 * (h + 1) * rows)
        for group, (slope_rows, text_rows) in zip(groups, spans):
            if h == 0:
                for copy in group:
                    copy.wait()
            share = lax.dot_general(
                slopes_held[slope_rows, columns], texts_held[text_rows, :],
                (((0,), (0,)), ((), ())), preferred_element_type=jnp.float32,
            )
            total = share if total is None else total + share
        if h == 0:
            for copy in groups[-1]:
                copy.wait()
        before_held[columns, :] = (before_held[columns, :] + total) * scalars[2]
        mine, other = ((c + 2 * h) * rows for c in (flags[4], 1 - flags[4]))
        here = slice(h * rows, (h + 1) * rows)
        kept[here, :] = before_held[pl.ds(pl.multiple_of(mine, rows), rows), :]
        gone = before_held[pl.ds(pl.multiple_of(other, rows), rows), :]
        sent[here, :] = gone.astype(jnp.bfloat16)
    g_right[...] = summed(sides[:rows, :], b_up[...])
    g_left[...] = summed(sides[rows:, :], b_down[...])
    loss = before_held[count:, :count]
    for line in lines:
        both = slopes_held[line, :].astype(jnp.float32)
        loss = loss + (both[:8] + both[8:])
    loss = jnp.sum(loss, axis=0, keepdims=True)
    write_losses(loss, sent, 2 * rows)
    kept[2 * rows :, :count] = jnp.broadcast_to(loss, (8, count))


def image_gradient(flags, scalars, rows, before, slopes, texts, near, b_up, b_down):
    width = texts[0].shape[1]
    count = slopes[0].shape[1]
    counts = [(s.shape[0] - 16) // rows for s in slopes]
    return call(
        functools.partial(image_kernel, counts), "image_gradient",
        [shaped(2 * rows + 16, width), shaped(2 * rows + 8, width, dtype=jnp.float32)]
        + [shaped(rows, width)] * 2,
        flags, scalars, before, near, b_up, b_down, *slopes, *texts,
        limit=56,
        in_specs=[SMEM] * 2 + [ANY] * 2 + [VMEM] * 2 + [ANY] * (len(slopes) + len(texts)),
        scratch=[
            pltpu.VMEM((count + 8, width), jnp.float32),
            pltpu.VMEM((sum(s.shape[0] for s in slopes), count), jnp.bfloat16),
            pltpu.VMEM((len(texts) * rows, width), jnp.bfloat16),
            pltpu.VMEM((2 * rows, width), jnp.bfloat16),
            pltpu.SemaphoreType.DMA((2 + len(slopes) + len(texts),)),
        ],
    )


def half_kernel(flags, kept, received, _, mine, sent, loss_out):
    rows, count = mine.shape[0], loss_out.shape[1]

    def summed_core(h):
        here = pl.ds(pl.multiple_of(h * rows, rows), rows)
        return kept[here, :] + received[here, :].astype(jnp.float32)

    mine[...] = summed_core(flags[3])
    sent[:rows] = summed_core(1 - flags[3]).astype(jnp.bfloat16)
    both = kept[2 * rows : 2 * rows + 1, :count] + read_losses(received, 2 * rows, count)
    loss_out[...] = both
    write_losses(both, sent, rows)


def loss_kernel(loss, received, _, out):
    out[...] = loss[...] + read_losses(received, received.shape[0] - 16, loss.shape[1])


def last_kernel(n, values, kept, *refs):
    grads, (out, kept_held, held, sems) = refs[:n], refs[-4:]
    rows = values.shape[0]
    half = rows // 4
    (copy,) = fetch([(kept, kept_held)], sems)
    inverses = inverse_norms(values[...].astype(jnp.float32))
    copy.wait()
    copies = []
    for j in range(4):
        here = slice(j * half, (j + 1) * half)
        wide = values[here, :].astype(jnp.float32)
        inverse = inverses[here, :]
        unit = wide * inverse
        grad = total_of(kept_held[here, :], *[g[here, :] for g in grads])
        along = jnp.sum(unit * grad, axis=1, keepdims=True)
        held[here, :] = (grad - unit * along) * inverse
        window = pl.ds(j * half, half)
        copies.append(
            pltpu.make_async_copy(held.at[window], out.at[window], sems.at[1 + j])
        )
        copies[-1].start()
    for copy in copies:
        copy.wait()


def projected(values, kept, *grads, after=()):
    rows, width = values.shape
    return call(
        functools.partial(last_kernel, len(grads)), "project",
        [shaped(rows, width, dtype=jnp.float32)],
        values, kept, *grads, *after,
        in_specs=[VMEM, ANY] + [VMEM] * len(grads) + [ANY] * len(after),
        out_specs=[ANY],
        scratch=[
            pltpu.VMEM((rows, width), kept.dtype),
            pltpu.VMEM((rows, width), jnp.float32),
            pltpu.SemaphoreType.DMA((5,)),
        ],
    )[0]


def total_of(*parts):
    total = parts[0].astype(jnp.float32)
    for part in parts[1:]:
        total = total + part.astype(jnp.float32)
    return total


def summed(*parts):
    return total_of(*parts).astype(jnp.bfloat16)


def on_device(picture_vectors, caption_vectors, scale_exponent, offset_addend):
    rows, width = caption_vectors.shape
    count = picture_vectors.shape[0]
    half = rows // 2
    b, rep = lax.axis_index("blk"), lax.axis_index("rep")
    x, q, h, c = b % 4, (b // 4) % 2, rep // 2, rep % 2
    scale = jnp.exp(scale_exponent)
    scalars = jnp.concatenate([scale * LOG2E, offset_addend * LOG2E, scale])
    first = (rep * rows).astype(jnp.int32)[None]
    flags = [(x == 0) & (q == 0), (x == 3) & (q == 1), (x >= 2) & (q == 1), h, c]
    flags = jnp.stack([flag.astype(jnp.int32) for flag in flags])
    kernel = functools.partial(pairs, scalars, first, rows)

    own = fetched_and_normalised(caption_vectors)
    outer = move(own, OUTER)
    right, left = move(own, RIGHT), move(own, LEFT)
    inner = move(own, FLIP)
    images = normalised(picture_vectors)
    block, piece = shaped(rows, width), shaped(half, width)
    packet = shaped(rows + half, width)
    (g_own,), total, flags = kernel(images, [own], own=(flags,), sums=1)
    to_left, to_right = call(
        pack_kernel, "pack", [packet, packet], flags, right, left, inner, outer, scalars=1,
    )
    from_right, from_left = move(to_left, RIGHT), move(to_right, LEFT)
    up, down = move(right, IN_UP), move(left, IN_DOWN)
    (g_near,), total = kernel(
        images, [right, left, inner, outer], joined=True, sums=2, before=(total,)
    )
    far, to_far = call(
        unpack_kernel, "unpack", [block] * 2,
        flags, g_near, from_right, from_left, inner, outer,
        in_specs=[SMEM, ANY] + [VMEM] * 4,
    )
    far_inner, far_outer = move(far, IN_FAR), move(to_far, OPPOSITE)
    (g_far, g_up, g_down, g_out_right, g_out_left), s_near = kernel(
        images, [far, up, down, from_right, from_left]
    )
    (g_far_inner, g_far_outer), s_far = kernel(
        images, [far_inner, far_outer], after=(s_near,)
    )

    def back(value, perm):
        return move(value, backwards(perm))

    b_up, b_down = back(g_up, IN_UP), back(g_down, IN_DOWN)
    b_out_right, b_out_left = back(g_out_right, RIGHT), back(g_out_left, LEFT)
    b_far_inner, b_far_outer = back(g_far_inner, IN_FAR), back(g_far_outer, OPPOSITE)
    held = [pltpu.VMEM((2 * rows, width), jnp.bfloat16), pltpu.SemaphoreType.DMA((1,))]
    sent, kept, g_right, g_left = image_gradient(
        flags, scalars, rows, total,
        [s_near, s_far],
        [far, up, down, from_right, from_left, far_inner, far_outer],
        g_near, b_up, b_down,
    )
    received = move(sent, CORE)
    wide = shaped(rows, width, dtype=jnp.float32)
    to_right, to_left = call(
        merge_far_kernel, "merge_far", [piece] * 2,
        b_far_inner, g_far, b_far_outer, b_out_right, b_out_left,
        in_specs=[VMEM] + [ANY] * 4,
        scratch=[pltpu.VMEM((rows, width), jnp.bfloat16), pltpu.SemaphoreType.DMA((1,))],
        flops=20_000_000_000,
    )
    g_inner, g_outer = call(
        merge_column_kernel, "merge_column", [block] * 2,
        flags, b_out_right, b_out_left, b_far_outer, g_near, to_left,
        in_specs=[SMEM] + [VMEM] * 3 + [ANY] * 2, scratch=held,
    )
    b_right, b_left = back(to_right, RIGHT), back(to_left, LEFT)
    mine, sent, loss = call(
        half_kernel, "half", [wide, shaped(rows + 16, width), shaped(1, count, dtype=jnp.float32)],
        flags, kept, received, to_left,
        in_specs=[SMEM, VMEM, VMEM, ANY],
    )
    received = move(sent, HALF)
    g_right, g_left = call(
        merge_near_kernel, "merge_near", [block] * 2, g_right, g_left, b_right, b_left
    )
    b_right, b_left = back(g_right, RIGHT), back(g_left, LEFT)
    b_inner, b_outer = back(g_inner, FLIP), back(g_outer, OUTER)
    pictures = lax.dynamic_slice_in_dim(picture_vectors, rep * rows, rows, 0)
    grad_images = projected(pictures, mine, received[:rows])
    (loss,) = call(
        loss_kernel, "losses", [loss], loss, received, grad_images, in_specs=[VMEM, VMEM, ANY]
    )
    loss_rows = lax.dynamic_slice_in_dim(loss[0], rep * rows, rows, 0) / (12 * count)
    grad_texts = projected(
        caption_vectors, g_own, b_right, b_left, b_inner, b_outer, after=(loss,)
    )
    return grad_images, grad_texts, loss_rows


def solution(mesh):
    in_specs = (P("blk", None), P(("blk", "rep"), None), P(), P())
    out_specs = (P(("blk", "rep"), None), P(("blk", "rep"), None), P(("blk", "rep")))
    return jax.shard_map(
        on_device, mesh=mesh, in_specs=in_specs, out_specs=out_specs, check_vma=False
    )
```
